256 devices in a mesh: ctx: 32 (over z_lo, x, core), exp: 8 (over y, z_hi).
Axes of the slice: x: 4, y: 4, z: 8 (z_hi: 2, z_lo: 4; z = z_hi * 4 + z_lo), core: 2. Of those that a mesh axis runs over, the one named last changes fastest.
Arguments:
- queries: bfloat16 [4096, 8192], P('ctx', 'exp'), may hold values from -6 to 6
- grad_heads: bfloat16 [4096, 8192], P('ctx', 'exp'), may hold values from -6 to 6
- latents: bfloat16 [4096, 512], P('ctx'), may hold values from -48 to 48
- w_uk: bfloat16 [512, 8192], P('ctx', 'exp'), may hold values from -0.25 to 0.25
- w_uv: bfloat16 [512, 8192], P('ctx', 'exp'), may hold values from -0.25 to 0.25
- moe_in: bfloat16 [4096, 7168], P('ctx', 'exp'), may hold values from -6 to 6
- grad_out: bfloat16 [4096, 7168], P('ctx', 'exp'), may hold values from -6 to 6
- routes: int32 [4096, 8], P('ctx'), may hold values from 0 to 255, as said below
- slots: int32 [4096, 8], P('ctx'), may hold values from -1 to 1, as said below
- gates: bfloat16 [4096, 8], P('ctx'), may hold values from 0.099609375 to 1
- w_gate: bfloat16 [32, 7168, 1024], P('ctx', None, 'exp'), may hold values from -0.0625 to 0.0625
- w_up: bfloat16 [32, 7168, 1024], P('ctx', None, 'exp'), may hold values from -0.0625 to 0.0625
- w_down: bfloat16 [32, 1024, 7168], P('ctx', 'exp'), may hold values from -0.1875 to 0.1875
Outputs:
- d_queries: bfloat16 [4096, 8192], P('ctx', 'exp')
- d_latents: float32 [4096, 512], P('ctx', 'exp')
- grad_w_uk: float32 [512, 8192], P('ctx', 'exp')
- grad_w_uv: float32 [512, 8192], P('ctx', 'exp')
- moe_grad: bfloat16 [4096, 7168], P('ctx', 'exp')
- gate_grads: float32 [4096, 8], P('ctx')
- grad_w_gate: bfloat16 [32, 7168, 1024], P('ctx', None, 'exp')
- grad_w_up: bfloat16 [32, 7168, 1024], P('ctx', None, 'exp')
- grad_w_down: bfloat16 [32, 1024, 7168], P('ctx', 'exp')
The draws below stay inside these ranges and needn't reach their ends.
Inputs may be any that keep to these rules, and one draw needn't show every extreme that they name: `routes`: each row names 8 different experts. One expert below 32 is named by every row. `slots`: for a route to an expert below 32: the number of earlier rows of the same aligned block of 128 rows (one device's tokens) that name that expert, if it is below 2; -1 otherwise and for routes to experts of 32 or above.
All inputs are finite; a program needn't handle non-finite values.
Results may differ from the reference program's by a relative error of at most 0.0085.
The reference program's roundings to bfloat16 on the way count: a program that leaves them out, or rounds other values in their place, can miss the bound.
Values may be sent and summed in bfloat16 or wider, within the bound.
A program may use at most 320 MiB of HBM per device.

```python
import math
import jax
import jax.numpy as jnp
from jax import lax

D = 7168
KVL = 512
HD = 128
EXPERTS = 256
TOP = 8
CAP = 2
TOK_DEV = 128
HEADS = 64
FF = 1024
WIN = 32
S = 4096
N_CTX = 32


def route_table(key):
    favourite_key, preference_key, jitter_key = jax.random.split(key, 3)
    favourite = jax.random.randint(favourite_key, (), 0, WIN)
    preference = jax.random.randint(preference_key, (EXPERTS,), 0, 4)
    jitter = jax.random.randint(jitter_key, (S, EXPERTS), 0, 4096)
    expert_ids = jnp.arange(EXPERTS, dtype=jnp.int32)
    ranking = (jitter + preference[None, :] * 1024) * EXPERTS + expert_ids[None, :]
    ranking = jnp.where(expert_ids[None, :] == favourite, 8192 * EXPERTS, ranking)
    ignored, chosen = lax.top_k(ranking, TOP)
    chosen = chosen.astype(jnp.int32)
    in_window = chosen < WIN
    onehot = jnp.sum((chosen[:, :, None] == jnp.arange(WIN, dtype=jnp.int32)[None, None, :]).astype(jnp.int32), axis=1)
    blocks = onehot.reshape(S // TOK_DEV, TOK_DEV, WIN)
    before = (jnp.cumsum(blocks, axis=1) - blocks).reshape(S, WIN)
    earlier = jnp.take_along_axis(before, jnp.minimum(chosen, WIN - 1), axis=1)
    slot_ids = jnp.where(in_window & (earlier < CAP), earlier, -1).astype(jnp.int32)
    return (chosen, slot_ids)


def draw_routes(key, part):
    chosen, slot_ids = route_table(key)
    return chosen


def draw_slots(key, part):
    chosen, slot_ids = route_table(key)
    return slot_ids


def draw_latents(key, part):
    key = jax.random.fold_in(key, 7)
    base_key, scale_key = jax.random.split(key)
    base_values = jax.random.normal(base_key, (S, KVL), jnp.float32)
    row_scale = jnp.exp(jax.random.uniform(scale_key, (S, 1), jnp.float32, math.log(0.5), math.log(2.0)))
    values = jnp.clip(base_values * row_scale, -12.0, 12.0)
    return values.astype(jnp.bfloat16)


def block_levels(key, shape, shards, least, top_value):
    gain = 1.0
    for axis_at, parts in shards:
        draws = jax.random.uniform(jax.random.fold_in(jax.random.fold_in(key, 6), axis_at), (parts,), jnp.float32, least / len(shards), top_value / len(shards))
        gain = gain * jnp.repeat(jnp.exp(draws), shape[axis_at] // parts).reshape((-1,) + (1,) * (len(shape) - 1 - axis_at))
    return gain


def gaussian(rng, shape, width, most, shards=(), kind=jnp.bfloat16):
    values = jax.random.normal(rng, shape, jnp.float32) * width
    if len(shards) > 0:
        values = block_levels(rng, shape, shards, -0.22, 0.18) * values
    return jnp.clip(values, min=-most, max=most).astype(kind)


def setup_inputs(seed: int = 0) -> dict:
    key_list = jax.random.split(jax.random.key(seed), 14)
    return {
        "queries": gaussian(key_list[0], (S, HEADS * HD), 1.0, 6.0, ((0, 32), (1, 8))),
        "grad_heads": gaussian(key_list[1], (S, HEADS * HD), 1.0, 6.0, ((0, 32), (1, 8))),
        "latents": draw_latents(jax.random.fold_in(key_list[13], 71), 0),
        "w_uk": gaussian(key_list[3], (KVL, HEADS * HD), KVL ** -0.5, 0.25, ((0, 32), (1, 8))),
        "w_uv": gaussian(key_list[4], (KVL, HEADS * HD), KVL ** -0.5, 0.25, ((0, 32), (1, 8))),
        "moe_in": gaussian(key_list[5], (S, D), 1.0, 6.0, ((0, 32), (1, 8))),
        "grad_out": gaussian(key_list[6], (S, D), 1.0, 6.0, ((0, 32), (1, 8))),
        "routes": draw_routes(jax.random.fold_in(key_list[13], 71), 0),
        "slots": draw_slots(jax.random.fold_in(key_list[13], 71), 0),
        "gates": jnp.clip(jnp.exp(math.log(1.0) - 2.306499 * jax.random.uniform(key_list[9], (S, TOP), jnp.float32) ** block_levels(key_list[9], (S, TOP), ((0, 32),), -0.2, 0.2)), 0.099609375, 1.0).astype(jnp.bfloat16),
        "w_gate": gaussian(key_list[10], (WIN, D, FF), D ** -0.5, 0.0625, ((0, 32), (2, 8))),
        "w_up": gaussian(key_list[11], (WIN, D, FF), D ** -0.5, 0.0625, ((0, 32), (2, 8))),
        "w_down": gaussian(key_list[12], (WIN, FF, D), FF ** -0.5, 0.1875, ((0, 32), (1, 8))),
    }


def attention_part(queries, grad_heads, latents, w_uk, w_uv):
    head_count = w_uk.shape[1] // HD
    scale_factor = HD ** -0.5
    positions = jnp.arange(S, dtype=jnp.int32)
    causal = positions[None, :] <= positions[:, None]
    query_split = queries.reshape(S, head_count, HD).transpose(1, 0, 2)
    grad_split = grad_heads.reshape(S, head_count, HD).transpose(1, 0, 2)
    key_split = w_uk.reshape(KVL, head_count, HD).transpose(1, 0, 2)
    value_split = w_uv.reshape(KVL, head_count, HD).transpose(1, 0, 2)

    def one_head(latent_grad, inputs):
        query_head, grad_head, key_head, value_head = inputs
        q_lat = jnp.dot(query_head, key_head.T, preferred_element_type=jnp.float32).astype(jnp.bfloat16)
        g_lat = jnp.dot(grad_head, value_head.T, preferred_element_type=jnp.float32).astype(jnp.bfloat16)
        scores = jnp.dot(q_lat, latents.T, preferred_element_type=jnp.float32) * scale_factor
        scores = jnp.where(causal, scores, -jnp.inf)
        top_score = jnp.max(scores, axis=1, keepdims=True)
        log_total = top_score + jnp.log(jnp.sum(jnp.exp(scores - top_score), axis=1, keepdims=True))
        prob_values = jnp.exp(scores - log_total)
        probs_low = prob_values.astype(jnp.bfloat16)
        o_lat = jnp.dot(probs_low, latents, preferred_element_type=jnp.float32)
        delta_sum = jnp.sum(g_lat.astype(jnp.float32) * o_lat, axis=1, keepdims=True)
        d_prob = jnp.dot(g_lat, latents.T, preferred_element_type=jnp.float32)
        d_score = (prob_values * (d_prob - delta_sum) * scale_factor).astype(jnp.bfloat16)
        dq_lat = jnp.dot(d_score, latents, preferred_element_type=jnp.float32).astype(jnp.bfloat16)
        d_query = jnp.dot(dq_lat, key_head, preferred_element_type=jnp.float32).astype(jnp.bfloat16)
        latent_grad = latent_grad + jnp.dot(d_score.T, q_lat, preferred_element_type=jnp.float32)
        latent_grad = latent_grad + jnp.dot(probs_low.T, g_lat, preferred_element_type=jnp.float32)
        key_grad = jnp.dot(dq_lat.T, query_head, preferred_element_type=jnp.float32)
        value_grad = jnp.dot(o_lat.astype(jnp.bfloat16).T, grad_head, preferred_element_type=jnp.float32)
        return latent_grad, (d_query, key_grad, value_grad)

    d_latents, outputs = lax.scan(one_head, jnp.zeros((S, KVL), jnp.float32),
                                  (query_split, grad_split, key_split, value_split))
    d_query, key_grad, value_grad = outputs
    d_queries = d_query.transpose(1, 0, 2).reshape(S, head_count * HD)
    grad_w_uk = key_grad.transpose(1, 0, 2).reshape(KVL, head_count * HD)
    grad_w_uv = value_grad.transpose(1, 0, 2).reshape(KVL, head_count * HD)
    return d_queries, d_latents, grad_w_uk, grad_w_uv


def expert_part(moe_in, grad_out, routes, slots, gates, w_gate, w_up, w_down):
    kept = slots >= 0
    token_block = jnp.arange(S, dtype=jnp.int32) // TOK_DEV
    slot_total = WIN * N_CTX * CAP
    placement_key = jnp.where(kept, (routes * N_CTX + token_block[:, None]) * CAP + slots, slot_total)
    flat_route = jnp.arange(S * TOP, dtype=jnp.int32).reshape(S, TOP)
    table = jnp.full((slot_total + 1,), -1, jnp.int32).at[placement_key.reshape(-1)].set(flat_route.reshape(-1))
    table = table[:slot_total].reshape(WIN, N_CTX * CAP)
    gate_flat = gates.reshape(-1)

    def one_expert(inputs):
        entries, gate_weight, up_weight, down_weight = inputs
        present = entries >= 0
        safe_entry = jnp.maximum(entries, 0)
        token_index = safe_entry // TOP
        rows_in = jnp.where(present[:, None], moe_in[token_index], jnp.zeros((), jnp.bfloat16))
        grads_in = jnp.where(present[:, None], grad_out[token_index], jnp.zeros((), jnp.bfloat16))
        gate_value = jnp.where(present, gate_flat[safe_entry].astype(jnp.float32), jnp.zeros((), jnp.float32))[:, None]
        hidden_gate = jnp.dot(rows_in, gate_weight, preferred_element_type=jnp.float32)
        hidden_up = jnp.dot(rows_in, up_weight, preferred_element_type=jnp.float32)
        sigmoid_gate = jax.nn.sigmoid(hidden_gate)
        activation = hidden_gate * sigmoid_gate * hidden_up
        act_grad = jnp.dot(grads_in, down_weight.T, preferred_element_type=jnp.float32)
        gate_term = jnp.sum(act_grad * activation, axis=1)
        scaled_grad = gate_value * act_grad
        scaled_act = (gate_value * activation).astype(jnp.bfloat16)
        down_grad = jnp.dot(scaled_act.T, grads_in, preferred_element_type=jnp.float32).astype(jnp.bfloat16)
        grad_gate_in = (scaled_grad * hidden_up * sigmoid_gate * (1.0 + hidden_gate * (1.0 - sigmoid_gate))).astype(jnp.bfloat16)
        grad_up_in = (scaled_grad * hidden_gate * sigmoid_gate).astype(jnp.bfloat16)
        gate_wgrad = jnp.dot(rows_in.T, grad_gate_in, preferred_element_type=jnp.float32).astype(jnp.bfloat16)
        up_wgrad = jnp.dot(rows_in.T, grad_up_in, preferred_element_type=jnp.float32).astype(jnp.bfloat16)
        row_grads = jnp.dot(grad_gate_in, gate_weight.T, preferred_element_type=jnp.float32)
        row_grads = row_grads + jnp.dot(grad_up_in, up_weight.T, preferred_element_type=jnp.float32)
        return gate_term, gate_wgrad, up_wgrad, down_grad, row_grads

    gate_term, grad_w_gate, grad_w_up, grad_w_down, row_grads = lax.map(one_expert, (table, w_gate, w_up, w_down))
    entries_flat = table.reshape(-1)
    present_flat = entries_flat >= 0
    token_all = jnp.where(present_flat, entries_flat // TOP, S)
    moe_grad = jax.ops.segment_sum(row_grads.reshape(-1, D), token_all, num_segments=S + 1)[:S].astype(jnp.bfloat16)
    route_all = jnp.where(present_flat, entries_flat, S * TOP)
    gate_grads = jax.ops.segment_sum(gate_term.reshape(-1), route_all, num_segments=S * TOP + 1)[:S * TOP].reshape(S, TOP)
    return moe_grad, gate_grads, grad_w_gate, grad_w_up, grad_w_down


def reference(queries, grad_heads, latents, w_uk, w_uv, moe_in, grad_out, routes, slots, gates, w_gate, w_up, w_down):
    d_queries, d_latents, grad_w_uk, grad_w_uv = attention_part(queries, grad_heads, latents, w_uk, w_uv)
    moe_grad, gate_grads, grad_w_gate, grad_w_up, grad_w_down = expert_part(
        moe_in, grad_out, routes, slots, gates, w_gate, w_up, w_down)
    return (d_queries, d_latents, grad_w_uk, grad_w_uv, moe_grad, gate_grads, grad_w_gate, grad_w_up, grad_w_down)
```

```python
import jax
import jax.numpy as jnp
from jax import lax
from jax.experimental import pallas as pl
from jax.experimental.pallas import tpu as pltpu
from jax.sharding import PartitionSpec as P

MESH = pl.DeviceIdType.MESH
HD = 128
CAP = 2
TOK = 128
NC = 32
F32 = jnp.float32
BF16 = jnp.bfloat16
DMA = pltpu.SemaphoreType.DMA
VMEM = pltpu.VMEM


class Place:
    def __init__(self):
        self.c = c = lax.axis_index("ctx")
        self.e = e = lax.axis_index("exp")
        self.z, self.x, self.core = c // 8, (c // 2) % 4, c % 2
        self.y, self.zh = e // 2, e % 2
        p = c % 8
        self.i = c // 4
        self.r = p + (p // 4) * (7 - 2 * p)

    def ctx(self, z, x, core):
        return (z * 8 + x * 2 + core, self.e)

    def exp(self, y, zh):
        return (self.c, y * 2 + zh)

    def member(self, i):
        return 4 * i + self.r + (i % 2) * (3 - 2 * self.r)


def greet(devices, loops):
    barrier = pltpu.get_barrier_semaphore()
    count = 0
    for steps, device in loops:

        def one(k, carry, device=device):
            pl.semaphore_signal(barrier, inc=1, device_id=device(k), device_id_type=MESH)
            return carry

        lax.fori_loop(0, steps, one, 0)
        count += steps
    for device in devices:
        pl.semaphore_signal(barrier, inc=1, device_id=device, device_id_type=MESH)
    pl.semaphore_wait(barrier, count + len(devices))


def send(src, dst, send_sem, recv_sem, device):
    copy = pltpu.make_async_remote_copy(
        src_ref=src,
        dst_ref=dst,
        send_sem=send_sem,
        recv_sem=recv_sem,
        device_id=device,
        device_id_type=MESH,
    )
    copy.start()
    return copy


def drain(ref, sem):
    pltpu.make_async_copy(ref, ref, sem).wait()


def ring_gather(at, pos, left, right, send_sem, recv_sem):
    other = (pos + 2) % 4
    before, after = (pos + 3) % 4, (pos + 1) % 4

    def first():
        for h in range(2):
            send(at(pos, h), at(pos, h), send_sem.at[h], recv_sem.at[h], right)
            send(at(pos, h), at(pos, h), send_sem.at[2 + h], recv_sem.at[2 + h], left)

    def second():
        drain(at(before, 0), recv_sem.at[0])
        send(at(before, 0), at(before, 0), send_sem.at[4], recv_sem.at[4], right)
        drain(at(after, 1), recv_sem.at[3])
        send(at(after, 1), at(after, 1), send_sem.at[5], recv_sem.at[5], left)

    def last():
        drain(at(before, 1), recv_sem.at[1])
        drain(at(after, 0), recv_sem.at[2])
        drain(at(other, 0), recv_sem.at[4])
        drain(at(other, 1), recv_sem.at[5])
        for k in range(6):
            drain(at(pos, 0), send_sem.at[k])

    return first, second, last


def ring_scatter(at, pos, left, right, held, send_sem, recv_sem, add):
    other = (pos + 2) % 4
    before, after = (pos + 3) % 4, (pos + 1) % 4

    def first():
        send(at(other, 0), held.at[0], send_sem.at[0], recv_sem.at[0], right)
        send(at(other, 1), held.at[1], send_sem.at[1], recv_sem.at[1], left)
        send(at(after, 1), held.at[3], send_sem.at[2], recv_sem.at[3], right)
        send(at(before, 0), held.at[4], send_sem.at[3], recv_sem.at[4], left)

    def second():
        drain(held.at[0], recv_sem.at[0])
        add(at(after, 0), held.at[0])
        send(at(after, 0), held.at[2], send_sem.at[4], recv_sem.at[2], right)
        drain(held.at[1], recv_sem.at[1])
        add(at(before, 1), held.at[1])
        send(at(before, 1), held.at[5], send_sem.at[5], recv_sem.at[5], left)

    def last():
        for k in range(2, 6):
            drain(held.at[k], recv_sem.at[k])
        for k in range(6):
            drain(held.at[k], send_sem.at[k])

    return first, second, last


def add_into(dst, src):
    def one(k, carry):
        dst[k] = (dst[k].astype(F32) + src[k].astype(F32)).astype(dst.dtype)
        return carry

    lax.fori_loop(0, dst.shape[0], one, 0)


def gather_kernel(
    q_ref, g_ref, wk_ref, wv_ref, lat_ref, moe_ref,
    qo, go, wko, wvo, lato, rowo,
    own_sem, send_sem, recv_sem, z_send, z_recv, x_send, x_recv, y_send, y_recv,
):
    at = Place()
    c, e = at.c, at.e
    left_x, right_x = at.ctx(at.z, (at.x + 3) % 4, at.core), at.ctx(at.z, (at.x + 1) % 4, at.core)
    left_y, right_y = at.exp((at.y + 3) % 4, at.zh), at.exp((at.y + 1) % 4, at.zh)
    twin, sibling = at.exp(at.y, 1 - at.zh), at.ctx(at.z, at.x, 1 - at.core)
    greet((left_y, right_y, twin), ((NC - 1, lambda k: ((c + 1 + k) % NC, e)),))

    def lanes(h):
        return pl.ds(pl.multiple_of(h * HD, HD), HD)

    rows16 = pl.ds(pl.multiple_of(c * 16, 16), 16)
    own = [
        pltpu.make_async_copy(moe_ref.at[c], rowo.at[e, c], own_sem.at[0]),
        pltpu.make_async_copy(lat_ref, lato.at[at.z, at.x, at.core], own_sem.at[1]),
        pltpu.make_async_copy(q_ref.at[:, lanes(at.i)], qo.at[at.i], own_sem.at[2]),
        pltpu.make_async_copy(g_ref.at[:, lanes(at.i)], go.at[at.i], own_sem.at[3]),
        pltpu.make_async_copy(wk_ref.at[:, lanes(at.i)], wko.at[rows16], own_sem.at[4]),
        pltpu.make_async_copy(wv_ref.at[:, lanes(at.i)], wvo.at[rows16], own_sem.at[5]),
    ]
    for copy in own:
        copy.start()

    def send_rows(k, carry):
        d = (c + 1 + k) % NC
        send(moe_ref.at[d], rowo.at[e, c], send_sem.at[0], recv_sem.at[0], (d, e))
        return carry

    lax.fori_loop(0, NC - 1, send_rows, 0)

    for k in range(1, 4):
        z = (at.z + k) % 4
        send(
            lat_ref, lato.at[at.z, at.x, at.core], z_send.at[k - 1], z_recv.at[k - 1],
            at.ctx(z, at.x, at.core),
        )

    def send_heads(k, carry):
        i = (at.i + 1 + k) % 8
        d = (at.member(i), e)
        send(q_ref.at[:, lanes(i)], qo.at[at.i], send_sem.at[1], recv_sem.at[1], d)
        send(g_ref.at[:, lanes(i)], go.at[at.i], send_sem.at[2], recv_sem.at[2], d)
        return carry

    lax.fori_loop(0, 7, send_heads, 0)

    def send_weights(k, carry):
        d = (c + 1 + k) % NC
        send(wk_ref.at[:, lanes(d // 4)], wko.at[rows16], send_sem.at[3], recv_sem.at[3], (d, e))
        send(wv_ref.at[:, lanes(d // 4)], wvo.at[rows16], send_sem.at[4], recv_sem.at[4], (d, e))
        return carry

    lax.fori_loop(0, NC - 1, send_weights, 0)

    own[0].wait()
    drain(rowo.at[e, pl.ds(0, NC - 1)], recv_sem.at[0])
    twin_copy = send(rowo.at[e], rowo.at[e], z_send.at[3], z_recv.at[3], twin)

    own[1].wait()
    for k in range(1, 4):
        drain(lat_ref, z_recv.at[k - 1])
    x_ring = ring_gather(
        lambda q, h: lato.at[pl.ds(2 * h, 2), q, at.core], at.x, left_x, right_x, x_send, x_recv
    )
    x_ring[0]()
    twin_copy.wait_recv()
    y_ring = ring_gather(
        lambda q, h: rowo.at[2 * q + h], at.y, left_y, right_y, y_send, y_recv
    )
    y_ring[0]()
    x_ring[1]()
    y_ring[1]()
    x_ring[2]()
    core_copy = send(
        lato.at[:, :, at.core], lato.at[:, :, at.core], z_send.at[4], z_recv.at[4], sibling
    )
    y_ring[2]()
    for copy in own[2:]:
        copy.wait()
    drain(rowo.at[e, pl.ds(0, NC - 1)], send_sem.at[0])
    for k, ref in ((1, qo), (2, go)):
        drain(ref.at[pl.ds(0, 7)], send_sem.at[k])
        drain(ref.at[pl.ds(0, 7)], recv_sem.at[k])
    for k, ref in ((3, wko), (4, wvo)):
        drain(ref.at[pl.ds(0, 16 * (NC - 1))], send_sem.at[k])
        drain(ref.at[pl.ds(0, 16 * (NC - 1))], recv_sem.at[k])
    for k in range(3):
        drain(lat_ref, z_send.at[k])
    twin_copy.wait_send()
    core_copy.wait()


def gather_inputs(queries, grad_heads, w_uk, w_uv, latents, messages):
    anywhere = pl.BlockSpec(memory_space=pl.ANY)
    depth = messages.shape[1]
    return pl.pallas_call(
        gather_kernel,
        out_shape=(
            jax.ShapeDtypeStruct((8, TOK, HD), BF16),
            jax.ShapeDtypeStruct((8, TOK, HD), BF16),
            jax.ShapeDtypeStruct((16 * NC, HD), BF16),
            jax.ShapeDtypeStruct((16 * NC, HD), BF16),
            jax.ShapeDtypeStruct((4, 4, 2, TOK, 512), BF16),
            jax.ShapeDtypeStruct((8, NC, depth, 128), BF16),
        ),
        in_specs=[anywhere] * 6,
        out_specs=(anywhere,) * 6,
        scratch_shapes=[
            DMA((6,)), DMA((5,)), DMA((5,)), DMA((5,)), DMA((5,)),
            DMA((6,)), DMA((6,)), DMA((6,)), DMA((6,)),
        ],
        compiler_params=pltpu.CompilerParams(collective_id=0, has_side_effects=True),
    )(queries, grad_heads, w_uk, w_uv, latents, messages)


def attention_kernel(
    q_ref, g_ref, wk_ref, wv_ref, lat_ref,
    dq_ref, kg_ref, vg_ref, dl_ref,
    lat_t, probs, dprob, low, tops, o_t, dq_t, dlat,
):
    r = Place().r
    scale = HD**-0.5
    width = 512
    contract_last = (((1,), (1,)), ((), ()))
    contract_first = (((0,), (0,)), ((), ()))

    def tile(t):
        return pl.ds(pl.multiple_of(t * width, width), width)

    def prepare(t, carry):
        lat_t[:, tile(t)] = lat_ref[tile(t), :].T
        dlat[tile(t), :] = jnp.zeros((width, 512), F32)
        return carry

    lax.fori_loop(0, 8, prepare, 0)
    kg_ref[...] = jnp.zeros_like(kg_ref)
    vg_ref[...] = jnp.zeros_like(vg_ref)
    column = lax.broadcasted_iota(jnp.int32, (1, 256), 1)
    key_at = lax.broadcasted_iota(jnp.int32, (width, 1), 0)

    def chunk(j, carry):
        rows = pl.ds(pl.multiple_of(j * 256, 256), 256)
        q, g = q_ref[rows, :], g_ref[rows, :]
        q_lat = lax.dot_general(q, wk_ref[...], contract_last, preferred_element_type=F32).astype(BF16)
        g_lat = lax.dot_general(g, wv_ref[...], contract_last, preferred_element_type=F32).astype(BF16)
        first_block = 8 * j + r
        second_block = 8 * j + 7 - r
        position = column + jnp.where(column < TOK, first_block * TOK, (second_block - 1) * TOK)
        o_t[...] = jnp.zeros_like(o_t)
        dq_t[...] = jnp.zeros_like(dq_t)

        def score(t, state):
            top, total = state
            keys = lat_ref[tile(t), :]
            s = lax.dot_general(keys, q_lat, contract_last, preferred_element_type=F32) * scale
            s = jnp.where(key_at + t * width <= position, s, -jnp.inf)
            new_top = jnp.maximum(top, jnp.max(s, axis=0, keepdims=True))
            weight = jnp.exp(s - new_top)
            probs[tile(t), :] = weight
            tops[t] = jnp.broadcast_to(new_top, (8, 256))
            dprob[tile(t), :] = lax.dot_general(keys, g_lat, contract_last, preferred_element_type=F32)
            total = total * jnp.exp(top - new_top) + jnp.sum(weight, axis=0, keepdims=True)
            return new_top, total

        top, total = lax.fori_loop(
            0, 2 * (j + 1), score, (jnp.full((1, 256), -1e30, F32), jnp.zeros((1, 256), F32))
        )
        inverse = 1.0 / total

        def output(t, delta):
            factor = jnp.exp(tops[t][0:1, :] - top) * inverse
            prob = probs[tile(t), :] * factor
            prob_low = prob.astype(BF16)
            probs[tile(t), :] = prob
            low[tile(t), :] = prob_low
            o_t[...] += jnp.dot(lat_t[:, tile(t)], prob_low, preferred_element_type=F32)
            return delta + jnp.sum(prob_low.astype(F32) * dprob[tile(t), :], axis=0, keepdims=True)

        delta = lax.fori_loop(0, 2 * (j + 1), output, jnp.zeros((1, 256), F32))

        def gradient(t, carry):
            dscore = (probs[tile(t), :] * (dprob[tile(t), :] - delta) * scale).astype(BF16)
            dq_t[...] += jnp.dot(lat_t[:, tile(t)], dscore, preferred_element_type=F32)
            dlat[tile(t), :] += jnp.dot(dscore, q_lat, preferred_element_type=F32) + jnp.dot(
                low[tile(t), :], g_lat, preferred_element_type=F32
            )
            return carry

        lax.fori_loop(0, 2 * (j + 1), gradient, 0)
        dq_low = dq_t[...].astype(BF16)
        dq_ref[rows, :] = lax.dot_general(
            dq_low, wk_ref[...], contract_first, preferred_element_type=F32
        ).astype(BF16)
        kg_ref[...] += jnp.dot(dq_low, q, preferred_element_type=F32)
        vg_ref[...] += jnp.dot(o_t[...].astype(BF16), g, preferred_element_type=F32)
        return carry

    lax.fori_loop(0, 4, chunk, 0)

    def finish(t, carry):
        dl_ref[tile(t), :] = dlat[tile(t), :].astype(BF16)
        return carry

    lax.fori_loop(0, 8, finish, 0)


def attention(q, g, wk, wv, lat):
    whole = pl.BlockSpec(memory_space=VMEM)
    return pl.pallas_call(
        attention_kernel,
        out_shape=(
            jax.ShapeDtypeStruct((1024, HD), BF16),
            jax.ShapeDtypeStruct((512, HD), F32),
            jax.ShapeDtypeStruct((512, HD), F32),
            jax.ShapeDtypeStruct((4096, 512), BF16),
        ),
        in_specs=[whole] * 5,
        out_specs=(whole,) * 4,
        scratch_shapes=[
            VMEM((512, 4096), BF16),
            VMEM((4096, 256), F32),
            VMEM((4096, 256), F32),
            VMEM((4096, 256), BF16),
            VMEM((8, 8, 256), F32),
            VMEM((512, 256), F32),
            VMEM((512, 256), F32),
            VMEM((4096, 512), F32),
        ],
        compiler_params=pltpu.CompilerParams(vmem_limit_bytes=56 * 1024 * 1024),
    )(q, g, wk, wv, lat)


def scatter_kernel(
    dl_ref, dq_ref, kg_ref, vg_ref, mb_ref,
    dqo, dlo, kgo, vgo, mo,
    part, core_held, x_held, y_part, y_held, z_part, z_held, m_part, m_held, twin_part, twin_held,
    m_send, kv_held,
    own_sem, send_sem, recv_sem, x_send, x_recv, y_send, y_recv, my_send, my_recv, z_send, z_recv,
):
    at = Place()
    c, e = at.c, at.e
    left_x, right_x = at.ctx(at.z, (at.x + 3) % 4, at.core), at.ctx(at.z, (at.x + 1) % 4, at.core)
    left_y, right_y = at.exp((at.y + 3) % 4, at.zh), at.exp((at.y + 1) % 4, at.zh)
    twin, sibling = at.exp(at.y, 1 - at.zh), at.ctx(at.z, at.x, 1 - at.core)

    def along_z(k):
        place = (at.zh * 4 + at.z + k) % 8
        return place // 4, place % 4, ((place % 4) * 8 + c % 8, at.y * 2 + place // 4)

    far = [
        (((at.z + k) % 4) * 8 + c % 8, at.y * 2 + 1 - at.zh) for k in range(1, 4)
    ]
    greet((left_y, right_y, twin, *far), ((NC - 1, lambda k: ((c + 1 + k) % NC, e)),))

    def lanes(h):
        return pl.ds(pl.multiple_of(h * HD, HD), HD)

    def rows16(d):
        return pl.ds(pl.multiple_of(d * 16, 16), 16)

    core_copy = send(dl_ref.at[:, :, 1 - at.core], core_held, send_sem.at[0], recv_sem.at[0], sibling)
    own = [
        pltpu.make_async_copy(dl_ref.at[:, :, at.core], part, own_sem.at[0]),
        pltpu.make_async_copy(mb_ref, m_part, own_sem.at[1]),
        pltpu.make_async_copy(dq_ref.at[at.i], dqo.at[:, lanes(at.i)], own_sem.at[2]),
        pltpu.make_async_copy(kg_ref.at[rows16(c)], kv_held.at[0, c], own_sem.at[3]),
        pltpu.make_async_copy(vg_ref.at[rows16(c)], kv_held.at[1, c], own_sem.at[4]),
    ]
    for copy in own:
        copy.start()
    own[1].wait()
    my_ring = ring_scatter(
        lambda q, h: m_part.at[2 * q + h], at.y, left_y, right_y, m_held, my_send, my_recv, add_into
    )
    my_ring[0]()

    def send_heads(k, carry):
        i = (at.i + 1 + k) % 8
        send(dq_ref.at[i], dqo.at[:, lanes(at.i)], send_sem.at[1], recv_sem.at[1], (at.member(i), e))
        return carry

    lax.fori_loop(0, 7, send_heads, 0)

    def send_weights(k, carry):
        d = (c + 1 + k) % NC
        send(kg_ref.at[rows16(d)], kv_held.at[0, c], send_sem.at[2], recv_sem.at[2], (d, e))
        send(vg_ref.at[rows16(d)], kv_held.at[1, c], send_sem.at[3], recv_sem.at[3], (d, e))
        return carry

    lax.fori_loop(0, NC - 1, send_weights, 0)

    own[0].wait()
    core_copy.wait_recv()

    def add_core(k, carry):
        add_into(part.at[k], core_held.at[k])
        return carry

    lax.fori_loop(0, 4, add_core, 0)
    x_ring = ring_scatter(
        lambda q, h: part.at[pl.ds(2 * h, 2), q], at.x, left_x, right_x, x_held, x_send, x_recv, add_into
    )
    x_ring[0]()
    my_ring[1]()
    x_ring[1]()
    my_ring[2]()

    def twin_out(k, carry):
        h = 1 - at.zh
        twin_part[k] = (
            m_part[2 * at.y + h, k].astype(F32) + m_held[2 + h, k].astype(F32) + m_held[4 + h, k].astype(F32)
        ).astype(BF16)
        return carry

    lax.fori_loop(0, NC, twin_out, 0)
    twin_copy = send(twin_part, twin_held, send_sem.at[4], recv_sem.at[4], twin)
    x_ring[2]()

    def x_sum(z, carry):
        total = part[z, at.x].astype(F32) + x_held[2 + z // 2, z % 2].astype(F32) + x_held[4 + z // 2, z % 2].astype(F32)
        low = total.astype(BF16)
        for q in range(4):
            y_part[q, z] = low[:, q * 128 : (q + 1) * 128]
        return carry

    lax.fori_loop(0, 4, x_sum, 0)
    y_ring = ring_scatter(
        lambda q, h: y_part.at[q, pl.ds(2 * h, 2)], at.y, left_y, right_y, y_held, y_send, y_recv, add_into
    )
    y_ring[0]()
    twin_copy.wait_recv()

    def twin_sum(k, carry):
        h = at.zh
        m_send[k] = (
            m_part[2 * at.y + h, k].astype(F32) + m_held[2 + h, k].astype(F32) + m_held[4 + h, k].astype(F32)
            + twin_held[k].astype(F32)
        )
        return carry

    lax.fori_loop(0, NC, twin_sum, 0)
    own_rows = pltpu.make_async_copy(m_send.at[c], mo.at[c], own_sem.at[5])
    own_rows.start()

    def send_rows(k, carry):
        d = (c + 1 + k) % NC
        send(m_send.at[d], mo.at[c], send_sem.at[5], recv_sem.at[5], (d, e))
        return carry

    lax.fori_loop(0, NC - 1, send_rows, 0)
    y_ring[1]()
    y_ring[2]()

    def y_sum(z, carry):
        z_part[z] = (
            y_part[at.y, z].astype(F32) + y_held[2 + z // 2, z % 2].astype(F32) + y_held[4 + z // 2, z % 2].astype(F32)
        )
        return carry

    lax.fori_loop(0, 4, y_sum, 0)
    for k in range(1, 8):
        _, z, device = along_z(k)
        send(z_part.at[z], z_held.at[k - 1], z_send.at[k - 1], z_recv.at[k - 1], device)

    own[3].wait()
    own[4].wait()
    drain(kv_held.at[0, pl.ds(0, NC - 1)], recv_sem.at[2])
    drain(kv_held.at[1, pl.ds(0, NC - 1)], recv_sem.at[3])
    for n, out in ((0, kgo), (1, vgo)):
        for h in range(8):
            out[:, h * HD : (h + 1) * HD] = (kv_held[n, 4 * h] + kv_held[n, 4 * h + 1]) + (
                kv_held[n, 4 * h + 2] + kv_held[n, 4 * h + 3]
            )
    for k in range(7):
        drain(z_held.at[k], z_recv.at[k])
    total = z_part[at.z]
    for k in range(7):
        total = total + z_held[k]
    dlo[...] = total

    for k in range(7):
        drain(z_held.at[k], z_send.at[k])
    own[2].wait()
    own_rows.wait()
    core_copy.wait_send()
    twin_copy.wait_send()
    drain(dq_ref.at[pl.ds(0, 7)], send_sem.at[1])
    drain(dq_ref.at[pl.ds(0, 7)], recv_sem.at[1])
    drain(kv_held.at[0, pl.ds(0, NC - 1)], send_sem.at[2])
    drain(kv_held.at[1, pl.ds(0, NC - 1)], send_sem.at[3])
    drain(m_send.at[pl.ds(0, NC - 1)], send_sem.at[5])
    drain(m_send.at[pl.ds(0, NC - 1)], recv_sem.at[5])


def scatter_outputs(dl, dq, kg, vg, mb):
    anywhere = pl.BlockSpec(memory_space=pl.ANY)
    whole = pl.BlockSpec(memory_space=VMEM)
    return pl.pallas_call(
        scatter_kernel,
        out_shape=(
            jax.ShapeDtypeStruct((TOK, 8 * HD), BF16),
            jax.ShapeDtypeStruct((TOK, 128), F32),
            jax.ShapeDtypeStruct((16, 8 * HD), F32),
            jax.ShapeDtypeStruct((16, 8 * HD), F32),
            jax.ShapeDtypeStruct((NC, 16, 128), F32),
        ),
        in_specs=[anywhere] * 5,
        out_specs=(anywhere, whole, whole, whole, anywhere),
        scratch_shapes=[
            VMEM((4, 4, TOK, 512), BF16),
            VMEM((4, 4, TOK, 512), BF16),
            VMEM((6, 2, TOK, 512), BF16),
            VMEM((4, 4, TOK, 128), BF16),
            VMEM((6, 2, TOK, 128), BF16),
            VMEM((4, TOK, 128), F32),
            VMEM((7, TOK, 128), F32),
            VMEM((8, NC, 16, 128), BF16),
            VMEM((6, NC, 16, 128), BF16),
            VMEM((NC, 16, 128), BF16),
            VMEM((NC, 16, 128), BF16),
            VMEM((NC, 16, 128), F32),
            VMEM((2, NC, 16, HD), F32),
            DMA((6,)), DMA((6,)), DMA((6,)), DMA((6,)), DMA((6,)), DMA((6,)), DMA((6,)),
            DMA((6,)), DMA((6,)), DMA((7,)), DMA((7,)),
        ],
        compiler_params=pltpu.CompilerParams(
            collective_id=1, has_side_effects=True, vmem_limit_bytes=56 * 1024 * 1024
        ),
    )(dl, dq, kg, vg, mb)


def on_device(
    queries, grad_heads, latents, w_uk, w_uv, moe_in, grad_out, routes, slots, gates, w_gate, w_up, w_down
):
    slot_count = NC * CAP
    destination = jnp.where(slots >= 0, routes * CAP + slots, -1)
    matches = (
        destination[:, :, None] == jnp.arange(slot_count, dtype=jnp.int32)[None, None, :]
    ).astype(F32)
    selector = jnp.sum(matches, axis=1)
    selector_low = selector.astype(BF16)
    pick = (((0,), (0,)), ((), ()))
    rows_send = lax.dot_general(selector_low, moe_in, pick, preferred_element_type=F32).astype(BF16)
    grads_send = lax.dot_general(selector_low, grad_out, pick, preferred_element_type=F32).astype(BF16)
    gate_send = jnp.sum(matches * gates.astype(F32)[:, :, None], axis=(0, 1)).astype(BF16)
    messages = jnp.concatenate(
        [
            rows_send.reshape(NC, 14, 128),
            grads_send.reshape(NC, 14, 128),
            jnp.broadcast_to(gate_send.reshape(NC, CAP, 1), (NC, CAP, 128)),
            jnp.zeros((NC, 2, 128), BF16),
        ],
        axis=1,
    )
    q, g, wk, wv, lat, rows = gather_inputs(queries, grad_heads, w_uk, w_uv, latents, messages)

    rows = rows.reshape(8, NC, 32, 128)

    def full(first):
        part = rows[:, :, first : first + 14].reshape(8, NC, CAP, 7, 128)
        return part.transpose(1, 2, 0, 3, 4).reshape(slot_count, 8 * 896)

    rows_flat, grads_flat = full(0), full(14)
    gate_column = rows[0, :, 28:30, 0].reshape(slot_count, 1).astype(F32)
    gate_weight, up_weight, down_weight = w_gate[0], w_up[0], w_down[0]
    last = (((1,), (1,)), ((), ()))
    hidden_gate = jnp.dot(rows_flat, gate_weight, preferred_element_type=F32)
    hidden_up = jnp.dot(rows_flat, up_weight, preferred_element_type=F32)
    sigmoid_gate = jax.nn.sigmoid(hidden_gate)
    activation = hidden_gate * sigmoid_gate * hidden_up
    act_grad = lax.dot_general(grads_flat, down_weight, last, preferred_element_type=F32)
    gate_part = jnp.sum(act_grad * activation, axis=1)
    scaled_grad = gate_column * act_grad
    scaled_act = (gate_column * activation).astype(BF16)
    down_grad = lax.dot_general(scaled_act, grads_flat, pick, preferred_element_type=F32).astype(BF16)
    grad_gate_in = (
        scaled_grad * hidden_up * sigmoid_gate * (1.0 + hidden_gate * (1.0 - sigmoid_gate))
    ).astype(BF16)
    grad_up_in = (scaled_grad * hidden_gate * sigmoid_gate).astype(BF16)
    gate_wgrad = lax.dot_general(rows_flat, grad_gate_in, pick, preferred_element_type=F32).astype(BF16)
    up_wgrad = lax.dot_general(rows_flat, grad_up_in, pick, preferred_element_type=F32).astype(BF16)
    row_grads = lax.dot_general(grad_gate_in, gate_weight, last, preferred_element_type=F32)
    row_grads = row_grads + lax.dot_general(grad_up_in, up_weight, last, preferred_element_type=F32)
    back = row_grads.astype(BF16).reshape(NC, CAP, 8, 7, 128).transpose(2, 0, 1, 3, 4).reshape(8, NC, 14, 128)
    gate_back = jnp.broadcast_to(gate_part.astype(BF16).reshape(1, NC, CAP, 1), (8, NC, CAP, 128))
    back = jnp.concatenate([back, gate_back], axis=2)

    dq, kg, vg, dl = attention(
        q.reshape(1024, HD), g.reshape(1024, HD), wk, wv, lat.reshape(4096, 512)
    )
    d_queries, d_latents, key_summed, value_summed, returned = scatter_outputs(
        dl.reshape(4, 4, 2, TOK, 512), dq.reshape(8, TOK, HD), kg, vg, back
    )
    d_latents = lax.dynamic_slice_in_dim(d_latents, (lax.axis_index("exp") % 2) * 64, 64, 1)
    moe_grad = jnp.dot(
        selector, returned[:, :14].reshape(slot_count, 896), precision=lax.Precision.HIGHEST
    ).astype(BF16)
    gate_grads = jnp.sum(matches * returned[:, 14:16, 0].reshape(1, 1, slot_count), axis=2)
    return (
        d_queries, d_latents, key_summed, value_summed, moe_grad, gate_grads,
        gate_wgrad[None], up_wgrad[None], down_grad[None],
    )


def solution(mesh):
    rows = P("ctx", "exp")
    in_specs = (
        rows, rows, P("ctx", None), rows, rows, rows, rows, P("ctx", None), P("ctx", None), P("ctx", None),
        P("ctx", None, "exp"), P("ctx", None, "exp"), P("ctx", "exp", None),
    )
    out_specs = (
        rows, rows, rows, rows, rows, P("ctx", None),
        P("ctx", None, "exp"), P("ctx", None, "exp"), P("ctx", "exp", None),
    )
    return jax.shard_map(on_device, mesh=mesh, in_specs=in_specs, out_specs=out_specs, check_vma=False)
```

```python
import jax
import jax.numpy as jnp
from jax import lax
from jax.experimental import pallas as pl
from jax.experimental.pallas import tpu as pltpu
from jax.sharding import PartitionSpec as P

MESH = pl.DeviceIdType.MESH
HD = 128
CAP = 2
TOK = 128
NC = 32
F32 = jnp.float32
BF16 = jnp.bfloat16
DMA = pltpu.SemaphoreType.DMA
VMEM = pltpu.VMEM


class Place:
    def __init__(self):
        self.c = c = lax.axis_index("ctx")
        self.e = e = lax.axis_index("exp")
        self.z, self.x, self.core = c // 8, (c // 2) % 4, c % 2
        self.y, self.zh = e // 2, e % 2
        p = c % 8
        self.i = c // 4
        self.r = p + (p // 4) * (7 - 2 * p)

    def ctx(self, z, x, core):
        return (z * 8 + x * 2 + core, self.e)

    def exp(self, y, zh):
        return (self.c, y * 2 + zh)

    def member(self, i):
        return 4 * i + self.r + (i % 2) * (3 - 2 * self.r)


def greet(devices, loops):
    barrier = pltpu.get_barrier_semaphore()
    count = 0
    for steps, device in loops:

        def one(k, carry, device=device):
            pl.semaphore_signal(barrier, inc=1, device_id=device(k), device_id_type=MESH)
            return carry

        lax.fori_loop(0, steps, one, 0)
        count += steps
    for device in devices:
        pl.semaphore_signal(barrier, inc=1, device_id=device, device_id_type=MESH)
    pl.semaphore_wait(barrier, count + len(devices))


def send(src, dst, send_sem, recv_sem, device):
    copy = pltpu.make_async_remote_copy(
        src_ref=src,
        dst_ref=dst,
        send_sem=send_sem,
        recv_sem=recv_sem,
        device_id=device,
        device_id_type=MESH,
    )
    copy.start()
    return copy


def drain(ref, sem):
    pltpu.make_async_copy(ref, ref, sem).wait()


def ring_gather(at, pos, left, right, send_sem, recv_sem):
    other = (pos + 2) % 4
    before, after = (pos + 3) % 4, (pos + 1) % 4

    def first():
        for h in range(2):
            send(at(pos, h), at(pos, h), send_sem.at[h], recv_sem.at[h], right)
            send(at(pos, h), at(pos, h), send_sem.at[2 + h], recv_sem.at[2 + h], left)

    def second():
        drain(at(before, 0), recv_sem.at[0])
        send(at(before, 0), at(before, 0), send_sem.at[4], recv_sem.at[4], right)
        drain(at(after, 1), recv_sem.at[3])
        send(at(after, 1), at(after, 1), send_sem.at[5], recv_sem.at[5], left)

    def last():
        drain(at(before, 1), recv_sem.at[1])
        drain(at(after, 0), recv_sem.at[2])
        drain(at(other, 0), recv_sem.at[4])
        drain(at(other, 1), recv_sem.at[5])
        for k in range(6):
            drain(at(pos, 0), send_sem.at[k])

    return first, second, last


def ring_scatter(at, pos, left, right, held, send_sem, recv_sem, add):
    other = (pos + 2) % 4
    before, after = (pos + 3) % 4, (pos + 1) % 4

    def first():
        send(at(other, 0), held.at[0], send_sem.at[0], recv_sem.at[0], right)
        send(at(other, 1), held.at[1], send_sem.at[1], recv_sem.at[1], left)
        send(at(after, 1), held.at[3], send_sem.at[2], recv_sem.at[3], right)
        send(at(before, 0), held.at[4], send_sem.at[3], recv_sem.at[4], left)

    def second():
        drain(held.at[0], recv_sem.at[0])
        add(at(after, 0), held.at[0])
        send(at(after, 0), held.at[2], send_sem.at[4], recv_sem.at[2], right)
        drain(held.at[1], recv_sem.at[1])
        add(at(before, 1), held.at[1])
        send(at(before, 1), held.at[5], send_sem.at[5], recv_sem.at[5], left)

    def last():
        for k in range(2, 6):
            drain(held.at[k], recv_sem.at[k])
        for k in range(6):
            drain(held.at[k], send_sem.at[k])

    return first, second, last


def add_into(dst, src):
    if len(dst.shape) == 2:
        dst[...] = (dst[...].astype(F32) + src[...].astype(F32)).astype(dst.dtype)
        return

    def one(k, carry):
        dst[k] = (dst[k].astype(F32) + src[k].astype(F32)).astype(dst.dtype)
        return carry

    lax.fori_loop(0, dst.shape[0], one, 0)


def fused_kernel(
    q_ref, g_ref, wk_ref, wv_ref, lat_ref, moe_ref, wg_ref, wu_ref, wd_ref,
    dqo, dlo, kgo, vgo, mo, gwgo, gwuo, gwdo,
    lat, lat_t, probs, dprob, tops, o_t, dq_t, dlat, qv, gv, wkv, wvv, dqv, kgv, vgv, kv_held,
    core_out, core_held, part, x_held, y_part, y_held, z_part, z_held,
    rows, spread, xs, ys, wg, wu, wd, gwg, gwu, gwd, dh, m_part, m_held, twin_part, twin_held, m_send,
    own_sem, send_sem, recv_sem, z_send, z_recv, ring_send, ring_recv, core_sem, last_send, last_recv,
):
    at = Place()
    c, e = at.c, at.e
    left_x, right_x = at.ctx(at.z, (at.x + 3) % 4, at.core), at.ctx(at.z, (at.x + 1) % 4, at.core)
    left_y, right_y = at.exp((at.y + 3) % 4, at.zh), at.exp((at.y + 1) % 4, at.zh)
    twin, sibling = at.exp(at.y, 1 - at.zh), at.ctx(at.z, at.x, 1 - at.core)
    far = [(((at.z + k) % 4) * 8 + c % 8, at.y * 2 + 1 - at.zh) for k in range(1, 4)]
    greet((left_y, right_y, twin, *far), ((NC - 1, lambda k: ((c + 1 + k) % NC, e)),))

    def lanes(h):
        return pl.ds(pl.multiple_of(h * HD, HD), HD)

    def rows16(d):
        return pl.ds(pl.multiple_of(d * 16, 16), 16)

    def gather_ring(n, pos, left, right, ref_at):
        return ring_gather(ref_at, pos, left, right, ring_send.at[n], ring_recv.at[n])

    def scatter_ring(n, pos, left, right, ref_at, held):
        return ring_scatter(ref_at, pos, left, right, held, ring_send.at[n], ring_recv.at[n], add_into)

    own = [
        pltpu.make_async_copy(moe_ref.at[c], rows.at[e, c], own_sem.at[0]),
        pltpu.make_async_copy(lat_ref.at[:, lanes(at.y)], lat.at[at.z, at.x, at.core, :, lanes(at.y)], own_sem.at[1]),
        pltpu.make_async_copy(q_ref.at[:, lanes(at.i)], qv.at[at.i], own_sem.at[2]),
        pltpu.make_async_copy(g_ref.at[:, lanes(at.i)], gv.at[at.i], own_sem.at[3]),
        pltpu.make_async_copy(wk_ref.at[:, lanes(at.i)], wkv.at[rows16(c)], own_sem.at[4]),
        pltpu.make_async_copy(wv_ref.at[:, lanes(at.i)], wvv.at[rows16(c)], own_sem.at[5]),
        pltpu.make_async_copy(wg_ref, wg, own_sem.at[6]),
        pltpu.make_async_copy(wu_ref, wu, own_sem.at[7]),
        pltpu.make_async_copy(wd_ref, wd, own_sem.at[8]),
    ]
    for k in (1, 0, 2, 3, 4, 5):
        own[k].start()
    lat_own = lat.at[at.z, at.x, at.core, :, lanes(at.y)]
    for k in range(1, 4):
        send(
            lat_ref.at[:, lanes(at.y)], lat_own, z_send.at[k - 1], z_recv.at[k - 1],
            at.ctx((at.z + k) % 4, at.x, at.core),
        )

    def send_rows(k, carry):
        d = (c + 1 + k) % NC
        send(moe_ref.at[d], rows.at[e, c], send_sem.at[0], recv_sem.at[0], (d, e))
        return carry

    lax.fori_loop(0, NC - 1, send_rows, 0)

    def send_heads(k, carry):
        i = (at.i + 1 + k) % 8
        d = (at.member(i), e)
        send(q_ref.at[:, lanes(i)], qv.at[at.i], send_sem.at[1], recv_sem.at[1], d)
        send(g_ref.at[:, lanes(i)], gv.at[at.i], send_sem.at[2], recv_sem.at[2], d)
        return carry

    lax.fori_loop(0, 7, send_heads, 0)

    def send_weights(k, carry):
        d = (c + 1 + k) % NC
        send(wk_ref.at[:, lanes(d // 4)], wkv.at[rows16(c)], send_sem.at[3], recv_sem.at[3], (d, e))
        send(wv_ref.at[:, lanes(d // 4)], wvv.at[rows16(c)], send_sem.at[4], recv_sem.at[4], (d, e))
        return carry

    lax.fori_loop(0, NC - 1, send_weights, 0)
    for k in (6, 7, 8):
        own[k].start()

    own[1].wait()
    for k in range(3):
        drain(lat_own, z_recv.at[k])
    xa = gather_ring(0, at.x, left_x, right_x, lambda q, h: lat.at[h, q, at.core, :, lanes(at.y)])
    yb = gather_ring(1, at.y, left_y, right_y, lambda q, h: lat.at[2 + h, at.x, at.core, :, lanes(q)])
    ya = gather_ring(2, at.y, left_y, right_y, lambda q, h: lat.at[h, :, at.core, :, lanes(q)])
    xb = gather_ring(3, at.x, left_x, right_x, lambda q, h: lat.at[2 + h, q, at.core])
    xa[0]()
    yb[0]()
    xa[1]()
    yb[1]()
    xa[2]()
    ya[0]()
    yb[2]()
    xb[0]()
    own[0].wait()
    drain(rows.at[e, pl.ds(0, NC - 1)], recv_sem.at[0])
    twin_in = send(rows.at[e], rows.at[e], z_send.at[3], z_recv.at[3], twin)
    ya[1]()
    xb[1]()
    ya[2]()
    core_a = send(lat.at[pl.ds(0, 2), :, at.core], lat.at[pl.ds(0, 2), :, at.core], z_send.at[4], z_recv.at[4], sibling)
    xb[2]()
    core_b = send(lat.at[pl.ds(2, 2), :, at.core], lat.at[pl.ds(2, 2), :, at.core], z_send.at[5], z_recv.at[5], sibling)
    for k in (2, 3, 4, 5):
        own[k].wait()
    for k, ref in ((1, qv), (2, gv)):
        drain(ref.at[pl.ds(0, 7)], recv_sem.at[k])
    for k, ref in ((3, wkv), (4, wvv)):
        drain(ref.at[pl.ds(0, 16 * (NC - 1))], recv_sem.at[k])
    core_a.wait_recv()

    scale = HD**-0.5
    contract_last = (((1,), (1,)), ((), ()))
    contract_first = (((0,), (0,)), ((), ()))
    width = 512

    def tile(t):
        return pl.ds(pl.multiple_of(t * width, width), width)

    def keys_at(t):
        return lat[t // 2, pl.ds(2 * (t % 2), 2)].reshape(width, 512)

    def turn(t, carry):
        lat_t[:, tile(t)] = keys_at(t).T
        return carry

    lax.fori_loop(0, 4, turn, 0)
    core_b.wait_recv()
    lax.fori_loop(4, 8, turn, 0)
    column = lax.broadcasted_iota(jnp.int32, (1, 256), 1)
    key_at = lax.broadcasted_iota(jnp.int32, (width, 1), 0)

    def chunk(j):
        q, g = qv[2 * j : 2 * j + 2].reshape(256, HD), gv[2 * j : 2 * j + 2].reshape(256, HD)
        q_lat = lax.dot_general(q, wkv[...], contract_last, preferred_element_type=F32).astype(BF16)
        g_lat = lax.dot_general(g, wvv[...], contract_last, preferred_element_type=F32).astype(BF16)
        position = column + jnp.where(column < TOK, (8 * j + at.r) * TOK, (8 * j + 6 - at.r) * TOK)
        o_t[...] = jnp.zeros_like(o_t)
        dq_t[...] = jnp.zeros_like(dq_t)

        def score(t, state, masked):
            top, total = state
            keys = keys_at(t)
            s = lax.dot_general(keys, q_lat, contract_last, preferred_element_type=F32) * scale
            if masked:
                s = jnp.where(key_at + t * width <= position, s, -jnp.inf)
            new_top = jnp.maximum(top, jnp.max(s, axis=0, keepdims=True))
            weight = jnp.exp(s - new_top)
            probs[tile(t), :] = weight
            tops[t] = jnp.broadcast_to(new_top, (8, 256))
            dprob[tile(t), :] = lax.dot_general(keys, g_lat, contract_last, preferred_element_type=F32)
            total = total * jnp.exp(top - new_top) + jnp.sum(weight, axis=0, keepdims=True)
            return new_top, total

        state = (jnp.full((1, 256), -1e30, F32), jnp.zeros((1, 256), F32))
        state = lax.fori_loop(0, 2 * j, lambda t, s: score(t, s, False), state)
        top, total = lax.fori_loop(2 * j, 2 * j + 2, lambda t, s: score(t, s, True), state)
        inverse = 1.0 / total

        def output(t, delta):
            prob = probs[tile(t), :] * (jnp.exp(tops[t][0:1, :] - top) * inverse)
            prob_low = prob.astype(BF16)
            probs[tile(t), :] = prob
            o_t[...] += jnp.dot(lat_t[:, tile(t)], prob_low, preferred_element_type=F32)
            return delta + jnp.sum(prob_low.astype(F32) * dprob[tile(t), :], axis=0, keepdims=True)

        delta = lax.fori_loop(0, 2 * j + 2, output, jnp.zeros((1, 256), F32))

        def gradient(t, carry):
            prob = probs[tile(t), :]
            dscore = (prob * (dprob[tile(t), :] - delta) * scale).astype(BF16)
            dq_t[...] += jnp.dot(lat_t[:, tile(t)], dscore, preferred_element_type=F32)
            step = jnp.dot(dscore, q_lat, preferred_element_type=F32) + jnp.dot(
                prob.astype(BF16), g_lat, preferred_element_type=F32
            )
            dlat[tile(t), :] = step if j == 3 else dlat[tile(t), :] + step
            return carry

        lax.fori_loop(0, 2 * j + 2, gradient, 0)
        dq_low = dq_t[...].astype(BF16)
        dq = lax.dot_general(dq_low, wkv[...], contract_first, preferred_element_type=F32).astype(BF16)
        dqv[2 * j : 2 * j + 2] = dq.reshape(2, TOK, HD)
        kg = jnp.dot(dq_low, q, preferred_element_type=F32)
        vg = jnp.dot(o_t[...].astype(BF16), g, preferred_element_type=F32)
        kgv[...] = kg if j == 3 else kgv[...] + kg
        vgv[...] = vg if j == 3 else vgv[...] + vg

    class Reduce:
        def __init__(self, b):
            self.b = b
            self.copy = None
            self.x_ring = scatter_ring(
                4 + b, at.x, left_x, right_x,
                lambda q, h: part.at[b, q, pl.ds(64 * h, 64)], x_held.at[b],
            )
            self.y_ring = scatter_ring(
                8 + b, at.y, left_y, right_y,
                lambda q, h: y_part.at[b, q, pl.ds(64 * h, 64)], y_held.at[b],
            )

        def block(self, x, core):
            return pl.ds(pl.multiple_of((self.b * 8 + x * 2 + core) * TOK, TOK), TOK)

        def to_core(self):
            b = self.b

            def one(x, carry):
                core_out[b, x] = dlat[self.block(x, 1 - at.core), :].astype(BF16)
                return carry

            lax.fori_loop(0, 4, one, 0)
            self.copy = send(core_out.at[b], core_held.at[b], core_sem.at[b], core_sem.at[4 + b], sibling)

        def x1(self):
            b = self.b
            self.copy.wait_recv()

            def one(x, carry):
                part[b, x] = (dlat[self.block(x, at.core), :] + core_held[b, x].astype(F32)).astype(BF16)
                return carry

            lax.fori_loop(0, 4, one, 0)
            self.x_ring[0]()

        def x2(self):
            self.x_ring[1]()

        def x3(self):
            b = self.b
            self.x_ring[2]()
            for h in range(2):
                half = pl.ds(64 * h, 64)
                total = (
                    part[b, at.x, half].astype(F32) + x_held[b, 2 + h].astype(F32) + x_held[b, 4 + h].astype(F32)
                ).astype(BF16)
                for q in range(4):
                    y_part[b, q, half] = total[:, q * 128 : (q + 1) * 128]
            self.y_ring[0]()

        def y2(self):
            self.y_ring[1]()

        def y3(self):
            b = self.b
            self.y_ring[2]()
            for h in range(2):
                half = pl.ds(64 * h, 64)
                z_part[b, half] = (
                    y_part[b, at.y, half].astype(F32) + y_held[b, 2 + h].astype(F32) + y_held[b, 4 + h].astype(F32)
                )

    rs = [Reduce(b) for b in range(4)]

    my = gather_ring(12, at.y, left_y, right_y, lambda q, h: rows.at[2 * q + h])
    mr = scatter_ring(13, at.y, left_y, right_y, lambda q, h: m_part.at[2 * q + h], m_held)

    def slice_lanes(n, f):
        return pl.ds(pl.multiple_of(n * 896 + f * 128, 128), 128)

    def slice_all(n):
        return pl.ds(pl.multiple_of(n * 896, 128), 896)

    def experts():
        for k in (6, 7, 8):
            own[k].wait()

        def unpack(n, carry):
            spread[...] = rows[n].reshape(1024, 128).astype(F32)
            for k in range(2):
                for f in range(7):
                    m = k * 7 + f
                    xs[32 * k : 32 * k + 32, slice_lanes(n, f)] = spread[pl.ds(m, 32, stride=32), :].astype(BF16)
                    ys[32 * k : 32 * k + 32, slice_lanes(n, f)] = spread[pl.ds(14 + m, 32, stride=32), :].astype(BF16)
            return carry

        lax.fori_loop(0, 8, unpack, 0)
        gate = jnp.concatenate([spread[pl.ds(28, 32, stride=32), :], spread[pl.ds(29, 32, stride=32), :]], axis=0)

        def hidden(n, sums):
            a, b, d = sums
            x, dy = xs[:, slice_all(n)], ys[:, slice_all(n)]
            a = a + jnp.dot(x, wg[slice_all(n), :], preferred_element_type=F32)
            b = b + jnp.dot(x, wu[slice_all(n), :], preferred_element_type=F32)
            d = d + lax.dot_general(dy, wd[:, slice_all(n)], contract_last, preferred_element_type=F32)
            return a, b, d

        zero = jnp.zeros((64, 128), F32)
        h1, h2, da = lax.fori_loop(0, 8, hidden, (zero, zero, zero))
        s = 1.0 / (1.0 + jnp.exp(-h1))
        act = h1 * s * h2
        gate_part = jnp.broadcast_to(jnp.sum(da * act, axis=1, keepdims=True), (64, 128))
        scaled = gate * da
        dh[0] = (gate * act).astype(BF16)
        dh[1] = (scaled * h2 * s * (1.0 + h1 * (1.0 - s))).astype(BF16)
        dh[2] = (scaled * h1 * s).astype(BF16)
        for k in range(2):
            spread[pl.ds(14 + k, 32, stride=16), :] = gate_part[32 * k : 32 * k + 32]

        def back(n, carry):
            dx = lax.dot_general(dh[1], wg[slice_all(n), :], contract_last, preferred_element_type=F32)
            dx = dx + lax.dot_general(dh[2], wu[slice_all(n), :], contract_last, preferred_element_type=F32)
            for k in range(2):
                for f in range(7):
                    spread[pl.ds(k * 7 + f, 32, stride=16), :] = dx[32 * k : 32 * k + 32, f * 128 : (f + 1) * 128]
            m_part[n] = spread[0:512, :].reshape(NC, 16, 128).astype(BF16)
            return carry

        lax.fori_loop(0, 8, back, 0)

    def weight_grads(out, k, dst, sem):
        def one(n, carry):
            out[slice_all(n), :] = lax.dot_general(
                xs[:, slice_all(n)], dh[k], contract_first, preferred_element_type=F32
            ).astype(BF16)
            return carry

        lax.fori_loop(0, 8, one, 0)
        copy = pltpu.make_async_copy(out, dst, sem)
        copy.start()
        return copy

    def down_grads():
        def one(n, carry):
            gwd[:, slice_all(n)] = lax.dot_general(
                dh[0], ys[:, slice_all(n)], contract_first, preferred_element_type=F32
            ).astype(BF16)
            return carry

        lax.fori_loop(0, 8, one, 0)
        copy = pltpu.make_async_copy(gwd, gwdo, own_sem.at[11])
        copy.start()
        return copy

    def y_total(h, k):
        return m_part[2 * at.y + h, k].astype(F32) + m_held[2 + h, k].astype(F32) + m_held[4 + h, k].astype(F32)

    def twin_out(k, carry):
        twin_part[k] = y_total(1 - at.zh, k).astype(BF16)
        return carry

    def twin_sum(k, carry):
        m_send[k] = y_total(at.zh, k) + twin_held[k].astype(F32)
        return carry

    def send_back(k, carry):
        d = (c + 1 + k) % NC
        send(m_send.at[d], mo.at[c], send_sem.at[5], recv_sem.at[5], (d, e))
        return carry

    def return_heads(k, carry):
        i = (at.i + 1 + k) % 8
        send(dqv.at[i], dqo.at[:, lanes(at.i)], send_sem.at[6], recv_sem.at[6], (at.member(i), e))
        return carry

    def return_weights(k, carry):
        d = (c + 1 + k) % NC
        send(kgv.at[rows16(d)], kv_held.at[0, c], send_sem.at[7], recv_sem.at[7], (d, e))
        send(vgv.at[rows16(d)], kv_held.at[1, c], send_sem.at[8], recv_sem.at[8], (d, e))
        return carry

    twin_in.wait_recv()
    my[0]()
    chunk(3)
    rs[3].to_core()
    my[1]()
    chunk(2)
    rs[3].x1()
    rs[2].to_core()
    my[2]()
    experts()
    mr[0]()
    chunk(1)
    rs[3].x2()
    rs[2].x1()
    rs[1].to_core()
    mr[1]()
    chunk(0)
    rs[0].to_core()
    lax.fori_loop(0, 7, return_heads, 0)
    lax.fori_loop(0, NC - 1, return_weights, 0)
    kept = [
        pltpu.make_async_copy(dqv.at[at.i], dqo.at[:, lanes(at.i)], own_sem.at[12]),
        pltpu.make_async_copy(kgv.at[rows16(c)], kv_held.at[0, c], own_sem.at[13]),
        pltpu.make_async_copy(vgv.at[rows16(c)], kv_held.at[1, c], own_sem.at[14]),
    ]
    for copy in kept:
        copy.start()
    mr[2]()
    lax.fori_loop(0, NC, twin_out, 0)
    twin_back = send(twin_part, twin_held, z_send.at[6], z_recv.at[6], twin)
    rs[2].x2()
    rs[1].x1()
    rs[3].x3()
    rs[0].x1()
    kept.append(down_grads())
    rs[1].x2()
    rs[3].y2()
    rs[2].x3()
    rs[0].x2()
    twin_back.wait_recv()
    lax.fori_loop(0, NC, twin_sum, 0)
    kept.append(pltpu.make_async_copy(m_send.at[c], mo.at[c], own_sem.at[15]))
    kept[-1].start()
    lax.fori_loop(0, NC - 1, send_back, 0)
    rs[1].x3()
    rs[0].x3()
    rs[3].y3()
    rs[2].y2()
    kept.append(weight_grads(gwg, 1, gwgo, own_sem.at[9]))
    rs[1].y2()
    rs[0].y2()
    kept.append(weight_grads(gwu, 2, gwuo, own_sem.at[10]))
    rs[2].y3()
    rs[1].y3()
    rs[0].y3()
    for k in range(1, 8):
        place = (at.zh * 4 + at.z + k) % 8
        z = place % 4
        device = (z * 8 + c % 8, at.y * 2 + place // 4)
        send(z_part.at[z], z_held.at[k - 1], last_send.at[k - 1], last_recv.at[k - 1], device)

    kept[1].wait()
    kept[2].wait()
    drain(kv_held.at[0, pl.ds(0, NC - 1)], recv_sem.at[7])
    drain(kv_held.at[1, pl.ds(0, NC - 1)], recv_sem.at[8])
    for n, out in ((0, kgo), (1, vgo)):
        for h in range(8):
            out[:, h * HD : (h + 1) * HD] = (kv_held[n, 4 * h] + kv_held[n, 4 * h + 1]) + (
                kv_held[n, 4 * h + 2] + kv_held[n, 4 * h + 3]
            )
    total = z_part[at.z]
    for k in range(7):
        drain(z_held.at[k], last_recv.at[k])
        total = total + z_held[k]
    dlo[...] = total

    kept[0].wait()
    for copy in kept[3:]:
        copy.wait()
    for k in range(7):
        drain(z_held.at[k], last_send.at[k])
    for b in range(4):
        rs[b].copy.wait_send()
    for copy in (twin_in, twin_back, core_a, core_b):
        copy.wait_send()
    for k in range(3):
        drain(lat_own, z_send.at[k])
    drain(rows.at[e, pl.ds(0, NC - 1)], send_sem.at[0])
    for k, ref in ((1, qv), (2, gv)):
        drain(ref.at[pl.ds(0, 7)], send_sem.at[k])
    for k, ref in ((3, wkv), (4, wvv)):
        drain(ref.at[pl.ds(0, 16 * (NC - 1))], send_sem.at[k])
    drain(m_send.at[pl.ds(0, NC - 1)], send_sem.at[5])
    drain(m_send.at[pl.ds(0, NC - 1)], recv_sem.at[5])
    drain(dqv.at[pl.ds(0, 7)], send_sem.at[6])
    drain(dqv.at[pl.ds(0, 7)], recv_sem.at[6])
    drain(kv_held.at[0, pl.ds(0, NC - 1)], send_sem.at[7])
    drain(kv_held.at[1, pl.ds(0, NC - 1)], send_sem.at[8])


def fused(queries, grad_heads, w_uk, w_uv, latents, messages, w_gate, w_up, w_down):
    anywhere = pl.BlockSpec(memory_space=pl.ANY)
    whole = pl.BlockSpec(memory_space=VMEM)
    shape = jax.ShapeDtypeStruct
    return pl.pallas_call(
        fused_kernel,
        out_shape=(
            shape((TOK, 8 * HD), BF16),
            shape((TOK, 128), F32),
            shape((16, 8 * HD), F32),
            shape((16, 8 * HD), F32),
            shape((NC, 16, 128), F32),
            shape((7168, 128), BF16),
            shape((7168, 128), BF16),
            shape((128, 7168), BF16),
        ),
        in_specs=[anywhere] * 9,
        out_specs=(anywhere, whole, whole, whole, anywhere, anywhere, anywhere, anywhere),
        scratch_shapes=[
            VMEM((4, 4, 2, TOK, 512), BF16),
            VMEM((512, 4096), BF16),
            VMEM((4096, 256), F32),
            VMEM((4096, 256), F32),
            VMEM((8, 8, 256), F32),
            VMEM((512, 256), F32),
            VMEM((512, 256), F32),
            VMEM((4096, 512), F32),
            VMEM((8, TOK, HD), BF16),
            VMEM((8, TOK, HD), BF16),
            VMEM((512, HD), BF16),
            VMEM((512, HD), BF16),
            VMEM((8, TOK, HD), BF16),
            VMEM((512, HD), F32),
            VMEM((512, HD), F32),
            VMEM((2, NC, 16, HD), F32),
            VMEM((4, 4, TOK, 512), BF16),
            VMEM((4, 4, TOK, 512), BF16),
            VMEM((4, 4, TOK, 512), BF16),
            VMEM((4, 6, 64, 512), BF16),
            VMEM((4, 4, TOK, 128), BF16),
            VMEM((4, 6, 64, 128), BF16),
            VMEM((4, TOK, 128), F32),
            VMEM((7, TOK, 128), F32),
            VMEM((8, NC, 32, 128), BF16),
            VMEM((1024, 128), F32),
            VMEM((64, 7168), BF16),
            VMEM((64, 7168), BF16),
            VMEM((7168, 128), BF16),
            VMEM((7168, 128), BF16),
            VMEM((128, 7168), BF16),
            VMEM((7168, 128), BF16),
            VMEM((7168, 128), BF16),
            VMEM((128, 7168), BF16),
            VMEM((3, 64, 128), BF16),
            VMEM((8, NC, 16, 128), BF16),
            VMEM((6, NC, 16, 128), BF16),
            VMEM((NC, 16, 128), BF16),
            VMEM((NC, 16, 128), BF16),
            VMEM((NC, 16, 128), F32),
            DMA((16,)), DMA((9,)), DMA((9,)), DMA((7,)), DMA((7,)),
            DMA((14, 6)), DMA((14, 6)), DMA((8,)), DMA((7,)), DMA((7,)),
        ],
        compiler_params=pltpu.CompilerParams(
            collective_id=0, has_side_effects=True, vmem_limit_bytes=62 * 1024 * 1024
        ),
    )(queries, grad_heads, w_uk, w_uv, latents, messages, w_gate, w_up, w_down)


def on_device(
    queries, grad_heads, latents, w_uk, w_uv, moe_in, grad_out, routes, slots, gates, w_gate, w_up, w_down
):
    slot_count = NC * CAP
    destination = jnp.where(slots >= 0, routes * CAP + slots, -1)
    matches = (
        destination[:, :, None] == jnp.arange(slot_count, dtype=jnp.int32)[None, None, :]
    ).astype(F32)
    selector = jnp.sum(matches, axis=1)
    selector_low = selector.astype(BF16)
    pick = (((0,), (0,)), ((), ()))
    rows_send = lax.dot_general(selector_low, moe_in, pick, preferred_element_type=F32).astype(BF16)
    grads_send = lax.dot_general(selector_low, grad_out, pick, preferred_element_type=F32).astype(BF16)
    gate_send = jnp.sum(matches * gates.astype(F32)[:, :, None], axis=(0, 1)).astype(BF16)
    messages = jnp.concatenate(
        [
            rows_send.reshape(NC, 14, 128),
            grads_send.reshape(NC, 14, 128),
            jnp.broadcast_to(gate_send.reshape(NC, CAP, 1), (NC, CAP, 128)),
            jnp.zeros((NC, 2, 128), BF16),
        ],
        axis=1,
    )
    d_queries, d_latents, key_summed, value_summed, returned, gate_wgrad, up_wgrad, down_grad = fused(
        queries, grad_heads, w_uk, w_uv, latents, messages, w_gate[0], w_up[0], w_down[0]
    )
    d_latents = lax.dynamic_slice_in_dim(d_latents, (lax.axis_index("exp") % 2) * 64, 64, 1)
    moe_grad = jnp.dot(
        selector, returned[:, :14].reshape(slot_count, 896), precision=lax.Precision.HIGHEST
    ).astype(BF16)
    gate_grads = jnp.sum(matches * returned[:, 14:16, 0].reshape(1, 1, slot_count), axis=2)
    return (
        d_queries, d_latents, key_summed, value_summed, moe_grad, gate_grads,
        gate_wgrad[None], up_wgrad[None], down_grad[None],
    )


def solution(mesh):
    rows = P("ctx", "exp")
    in_specs = (
        rows, rows, P("ctx", None), rows, rows, rows, rows, P("ctx", None), P("ctx", None), P("ctx", None),
        P("ctx", None, "exp"), P("ctx", None, "exp"), P("ctx", "exp", None),
    )
    out_specs = (
        rows, rows, rows, rows, rows, P("ctx", None),
        P("ctx", None, "exp"), P("ctx", None, "exp"), P("ctx", "exp", None),
    )
    return jax.shard_map(on_device, mesh=mesh, in_specs=in_specs, out_specs=out_specs, check_vma=False)
```

```python
import jax
import jax.numpy as jnp
from jax import lax
from jax.experimental import pallas as pl
from jax.experimental.pallas import tpu as pltpu
from jax.sharding import PartitionSpec as P

MESH = pl.DeviceIdType.MESH
HD = 128
CAP = 2
TOK = 128
NC = 32
F32 = jnp.float32
BF16 = jnp.bfloat16
DMA = pltpu.SemaphoreType.DMA
VMEM = pltpu.VMEM


class Place:
    def __init__(self):
        self.c = c = lax.axis_index("ctx")
        self.e = e = lax.axis_index("exp")
        self.z, self.x, self.core = c // 8, (c // 2) % 4, c % 2
        self.y, self.zh = e // 2, e % 2
        p = c % 8
        self.i = c // 4
        self.r = p + (p // 4) * (7 - 2 * p)

    def ctx(self, z, x, core):
        return (z * 8 + x * 2 + core, self.e)

    def exp(self, y, zh):
        return (self.c, y * 2 + zh)

    def member(self, i):
        return 4 * i + self.r + (i % 2) * (3 - 2 * self.r)


def greet(devices, loops):
    barrier = pltpu.get_barrier_semaphore()
    count = 0
    for steps, device in loops:

        def one(k, carry, device=device):
            pl.semaphore_signal(barrier, inc=1, device_id=device(k), device_id_type=MESH)
            return carry

        lax.fori_loop(0, steps, one, 0)
        count += steps
    for device in devices:
        pl.semaphore_signal(barrier, inc=1, device_id=device, device_id_type=MESH)
    pl.semaphore_wait(barrier, count + len(devices))


def send(src, dst, send_sem, recv_sem, device):
    copy = pltpu.make_async_remote_copy(
        src_ref=src,
        dst_ref=dst,
        send_sem=send_sem,
        recv_sem=recv_sem,
        device_id=device,
        device_id_type=MESH,
    )
    copy.start()
    return copy


def drain(ref, sem):
    pltpu.make_async_copy(ref, ref, sem).wait()


def ring_gather(at, pos, left, right, send_sem, recv_sem):
    other = (pos + 2) % 4
    before, after = (pos + 3) % 4, (pos + 1) % 4

    def first():
        for h in range(2):
            send(at(pos, h), at(pos, h), send_sem.at[h], recv_sem.at[h], right)
            send(at(pos, h), at(pos, h), send_sem.at[2 + h], recv_sem.at[2 + h], left)

    def second():
        drain(at(before, 0), recv_sem.at[0])
        send(at(before, 0), at(before, 0), send_sem.at[4], recv_sem.at[4], right)
        drain(at(after, 1), recv_sem.at[3])
        send(at(after, 1), at(after, 1), send_sem.at[5], recv_sem.at[5], left)

    def last(arrived=lambda k, q: None):
        drain(at(before, 1), recv_sem.at[1])
        arrived(1, before)
        drain(at(after, 0), recv_sem.at[2])
        arrived(2, after)
        drain(at(other, 0), recv_sem.at[4])
        drain(at(other, 1), recv_sem.at[5])
        arrived(3, other)
        for k in range(6):
            drain(at(pos, 0), send_sem.at[k])

    return first, second, last


def ring_scatter(at, pos, left, right, held, send_sem, recv_sem, add):
    other = (pos + 2) % 4
    before, after = (pos + 3) % 4, (pos + 1) % 4

    def first():
        send(at(other, 0), held.at[0], send_sem.at[0], recv_sem.at[0], right)
        send(at(other, 1), held.at[1], send_sem.at[1], recv_sem.at[1], left)
        send(at(after, 1), held.at[3], send_sem.at[2], recv_sem.at[3], right)
        send(at(before, 0), held.at[4], send_sem.at[3], recv_sem.at[4], left)

    def second():
        drain(held.at[0], recv_sem.at[0])
        add(at(after, 0), held.at[0])
        send(at(after, 0), held.at[2], send_sem.at[4], recv_sem.at[2], right)
        drain(held.at[1], recv_sem.at[1])
        add(at(before, 1), held.at[1])
        send(at(before, 1), held.at[5], send_sem.at[5], recv_sem.at[5], left)

    def last():
        for k in range(2, 6):
            drain(held.at[k], recv_sem.at[k])
        for k in range(6):
            drain(held.at[k], send_sem.at[k])

    return first, second, last


def add_into(dst, src):
    if len(dst.shape) == 2:
        dst[...] = (dst[...].astype(F32) + src[...].astype(F32)).astype(dst.dtype)
        return

    def one(k, carry):
        dst[k] = (dst[k].astype(F32) + src[k].astype(F32)).astype(dst.dtype)
        return carry

    lax.fori_loop(0, dst.shape[0], one, 0)


def fused_kernel(
    q_ref, g_ref, wk_ref, wv_ref, lat_ref, moe_ref, wg_ref, wu_ref, wd_ref,
    dqo, dlo, kgo, vgo, mo, gwgo, gwuo, gwdo,
    lat, lat_t, probs, dprob, tops, o_t, dq_t, dlat, qv, gv, w4, wkv, wvv, dqv, kgv, vgv, kq, kr, ks, kv_held,
    core_out, core_held, part, x_held, y_part, y_held, z_part, z_held,
    rows, spread, xs, ys, wg, wu, wd, gwg, gwu, gwd, dh, m_part, m_held, m_send, gate_sum,
    own_sem, send_sem, recv_sem, z_send, z_recv, ring_send, ring_recv, core_sem, last_send, last_recv,
    piece_send, piece_recv, local_send, local_recv,
):
    at = Place()
    c, e = at.c, at.e
    left_x, right_x = at.ctx(at.z, (at.x + 3) % 4, at.core), at.ctx(at.z, (at.x + 1) % 4, at.core)
    left_y, right_y = at.exp((at.y + 3) % 4, at.zh), at.exp((at.y + 1) % 4, at.zh)
    sibling = at.ctx(at.z, at.x, 1 - at.core)
    e_far = at.y * 2 + 1 - at.zh
    greet(
        [at.exp((at.y + k) % 4, at.zh) for k in range(1, 4)],
        ((NC - 1, lambda k: ((c + 1 + k) % NC, e)), (NC, lambda k: ((c + k) % NC, e_far))),
    )

    def lanes(h):
        return pl.ds(pl.multiple_of(h * HD, HD), HD)

    def local(k):
        p = (c % 4 + k) % 4
        return (4 * at.i + p, e), p + (at.i % 2) * (3 - 2 * p)

    def gather_ring(n, pos, left, right, ref_at):
        return ring_gather(ref_at, pos, left, right, ring_send.at[n], ring_recv.at[n])

    def scatter_ring(n, pos, left, right, ref_at, held):
        return ring_scatter(ref_at, pos, left, right, held, ring_send.at[n], ring_recv.at[n], add_into)

    own = [
        pltpu.make_async_copy(moe_ref.at[c], rows.at[e, c], own_sem.at[0]),
        pltpu.make_async_copy(lat_ref.at[:, lanes(at.y)], lat.at[at.z, at.x, at.core, :, lanes(at.y)], own_sem.at[1]),
        pltpu.make_async_copy(q_ref.at[:, lanes(at.i)], qv.at[at.i], own_sem.at[2]),
        pltpu.make_async_copy(g_ref.at[:, lanes(at.i)], gv.at[at.i], own_sem.at[3]),
        pltpu.make_async_copy(wk_ref.at[:, lanes(at.i)], w4.at[at.r, 0, at.i], own_sem.at[4]),
        pltpu.make_async_copy(wv_ref.at[:, lanes(at.i)], w4.at[at.r, 1, at.i], own_sem.at[5]),
        pltpu.make_async_copy(wg_ref, wg, own_sem.at[6]),
        pltpu.make_async_copy(wu_ref, wu, own_sem.at[7]),
        pltpu.make_async_copy(wd_ref, wd, own_sem.at[8]),
    ]
    for k in (1, 0, 2, 3, 4, 5):
        own[k].start()
    lat_own = lat.at[at.z, at.x, at.core, :, lanes(at.y)]
    for k in range(1, 4):
        send(
            lat_ref.at[:, lanes(at.y)], lat_own, z_send.at[k - 1], z_recv.at[k - 1],
            at.ctx((at.z + k) % 4, at.x, at.core),
        )

    def send_rows(k, carry):
        d = (c + 1 + k) % NC
        send(moe_ref.at[d], rows.at[e, c], send_sem.at[0], recv_sem.at[0], (d, e))
        send(moe_ref.at[d], rows.at[e, c], send_sem.at[9], recv_sem.at[9], (d, e_far))
        return carry


    def send_weights(k, carry):
        i = (at.i + 1 + k) % 8
        d = (at.member(i), e)
        send(wk_ref.at[:, lanes(i)], w4.at[at.r, 0, at.i], send_sem.at[3], recv_sem.at[3], d)
        send(wv_ref.at[:, lanes(i)], w4.at[at.r, 1, at.i], send_sem.at[4], recv_sem.at[4], d)
        return carry

    def send_heads(k, carry):
        i = (at.i + 1 + k) % 8
        d = (at.member(i), e)
        send(q_ref.at[:, lanes(i)], qv.at[at.i], send_sem.at[1], recv_sem.at[1], d)
        send(g_ref.at[:, lanes(i)], gv.at[at.i], send_sem.at[2], recv_sem.at[2], d)
        return carry

    for k in (6, 7, 8):
        own[k].start()

    own[1].wait()
    for k in range(3):
        drain(lat_own, z_recv.at[k])
    xa = gather_ring(0, at.x, left_x, right_x, lambda q, h: lat.at[h, q, at.core, :, lanes(at.y)])
    yb = gather_ring(1, at.y, left_y, right_y, lambda q, h: lat.at[2 + h, at.x, at.core, :, lanes(q)])
    ya = gather_ring(2, at.y, left_y, right_y, lambda q, h: lat.at[h, :, at.core, :, lanes(q)])
    xb = gather_ring(3, at.x, left_x, right_x, lambda q, h: lat.at[2 + h, q, at.core])
    xa[0]()
    yb[0]()
    lax.fori_loop(0, 7, send_heads, 0)
    lax.fori_loop(0, 7, send_weights, 0)
    xa[1]()
    yb[1]()

    def piece_a(k, q):
        ref = lat.at[pl.ds(0, 2), :, at.core, :, lanes(q)]
        send(ref, ref, piece_send.at[k], piece_recv.at[k], sibling)

    def piece_b(k, q):
        ref = lat.at[pl.ds(2, 2), q, at.core]
        send(ref, ref, piece_send.at[4 + k], piece_recv.at[4 + k], sibling)

    xa[2]()
    ya[0]()
    piece_a(0, at.y)
    yb[2]()
    xb[0]()
    piece_b(0, at.x)
    lax.fori_loop(0, NC - 1, send_rows, 0)
    send(moe_ref.at[c], rows.at[e, c], send_sem.at[9], recv_sem.at[9], (c, e_far))
    ya[1]()
    xb[1]()
    for k in (4, 5):
        own[k].wait()
    for k in (3, 4):
        drain(w4.at[at.r, k - 3, pl.ds(0, 7)], recv_sem.at[k])
    for k in range(1, 4):
        send(w4.at[at.r], w4.at[at.r], local_send.at[k - 1], local_recv.at[k - 1], local(k)[0])
    ya[2](piece_a)
    xb[2](piece_b)
    for k in range(3):
        drain(w4.at[at.r], local_recv.at[k])
    for i in range(8):
        for p in range(4):
            group = p if i % 2 == 0 else 3 - p
            rows16 = pl.ds(16 * (4 * i + p), 16)
            wkv[rows16] = w4[group, 0, i]
            wvv[rows16] = w4[group, 1, i]
    for k in (2, 3):
        own[k].wait()
    for k, ref in ((1, qv), (2, gv)):
        drain(ref.at[pl.ds(0, 7)], recv_sem.at[k])

    my = gather_ring(12, at.y, left_y, right_y, lambda q, h: rows.at[2 * q + h])
    mr = scatter_ring(13, at.y, left_y, right_y, lambda q, h: m_part.at[2 * q + h], m_held)

    def rows_here():
        own[0].wait()
        drain(rows.at[e, pl.ds(0, NC - 1)], recv_sem.at[0])
        drain(rows.at[e_far], recv_sem.at[9])
        my[0]()

    scale = HD**-0.5
    fast = scale * 1.4426950408889634
    contract_last = (((1,), (1,)), ((), ()))
    contract_first = (((0,), (0,)), ((), ()))
    width = 512

    def tile(t):
        return pl.ds(pl.multiple_of(t * width, width), width)

    def keys_at(t):
        return lat[t // 2, pl.ds(2 * (t % 2), 2)].reshape(width, 512)

    def pieces(first):
        for k in range(first, first + 4):
            drain(lat.at[pl.ds(0, 2), :, 0, :, pl.ds(0, 128)], piece_recv.at[k])

    pieces(0)
    column = lax.broadcasted_iota(jnp.int32, (1, 256), 1)
    key_at = lax.broadcasted_iota(jnp.int32, (width, 1), 0)

    def chunk(j, after_score=(), after_output=()):
        q, g = qv[2 * j : 2 * j + 2].reshape(256, HD), gv[2 * j : 2 * j + 2].reshape(256, HD)
        q_lat = lax.dot_general(q, wkv[...], contract_last, preferred_element_type=F32).astype(BF16)
        g_lat = lax.dot_general(g, wvv[...], contract_last, preferred_element_type=F32).astype(BF16)
        position = column + jnp.where(column < TOK, (8 * j + at.r) * TOK, (8 * j + 6 - at.r) * TOK)

        def score(b, state, masked):
            top, total = state
            raw = []
            for t in (2 * b, 2 * b + 1):
                keys = keys_at(t)
                if j == 3:
                    lat_t[:, tile(t)] = keys.T
                s = lax.dot_general(keys, q_lat, contract_last, preferred_element_type=F32)
                if masked:
                    s = jnp.where(key_at + t * width <= position, s, -jnp.inf)
                raw.append(s)
                dprob[tile(t), :] = lax.dot_general(keys, g_lat, contract_last, preferred_element_type=F32)
            new_top = jnp.maximum(top, jnp.max(jnp.maximum(raw[0], raw[1]), axis=0, keepdims=True))
            total = total * jnp.exp2((top - new_top) * fast)
            for u in range(2):
                weight = jnp.exp2((raw[u] - new_top) * fast)
                probs[tile(2 * b + u), :] = weight
                total = total + jnp.sum(weight, axis=0, keepdims=True)
            tops[b] = jnp.broadcast_to(new_top, (8, 256))
            return new_top, total

        state = (jnp.full((1, 256), -1e30, F32), jnp.zeros((1, 256), F32))
        if j == 3:
            state = lax.fori_loop(0, 2, lambda b, s: score(b, s, False), state)
            pieces(4)
            state = score(2, state, False)
        elif j > 0:
            state = lax.fori_loop(0, j, lambda b, s: score(b, s, False), state)
        top, total = score(j, state, True)
        inverse = 1.0 / total
        for step in after_score:
            step()
        o_t[...] = jnp.zeros_like(o_t)
        dq_t[...] = jnp.zeros_like(dq_t)

        def output(b, delta):
            factor = jnp.exp2((tops[b][0:1, :] - top) * fast) * inverse
            sum_o = o_t[...]
            for t in (2 * b, 2 * b + 1):
                prob_low = (probs[tile(t), :] * factor).astype(BF16)
                sum_o = sum_o + jnp.dot(lat_t[:, tile(t)], prob_low, preferred_element_type=F32)
                delta = delta + jnp.sum(prob_low.astype(F32) * dprob[tile(t), :], axis=0, keepdims=True)
            o_t[...] = sum_o
            return delta

        delta = lax.fori_loop(0, j + 1, output, jnp.zeros((1, 256), F32))
        for step in after_output:
            step()

        def gradient(b, carry):
            factor = jnp.exp2((tops[b][0:1, :] - top) * fast) * inverse
            sum_q = dq_t[...]
            for t in (2 * b, 2 * b + 1):
                prob = probs[tile(t), :] * factor
                dscore = (prob * (dprob[tile(t), :] - delta) * scale).astype(BF16)
                sum_q = sum_q + jnp.dot(lat_t[:, tile(t)], dscore, preferred_element_type=F32)
                step = jnp.dot(dscore, q_lat, preferred_element_type=F32) + jnp.dot(
                    prob.astype(BF16), g_lat, preferred_element_type=F32
                )
                dlat[tile(t), :] = step if j == 3 else dlat[tile(t), :] + step
            dq_t[...] = sum_q
            return carry

        lax.fori_loop(0, j + 1, gradient, 0)
        dq_low = dq_t[...].astype(BF16)
        dq = lax.dot_general(dq_low, wkv[...], contract_first, preferred_element_type=F32).astype(BF16)
        dqv[2 * j : 2 * j + 2] = dq.reshape(2, TOK, HD)
        kg = jnp.dot(dq_low, q, preferred_element_type=F32)
        vg = jnp.dot(o_t[...].astype(BF16), g, preferred_element_type=F32)
        kgv[...] = kg if j == 3 else kgv[...] + kg
        vgv[...] = vg if j == 3 else vgv[...] + vg
        for n in (2 * j, 2 * j + 1):
            block = dqo.at[:, lanes(at.i)]

            @pl.when(at.i == n)
            def _():
                pltpu.make_async_copy(dqv.at[n], block, own_sem.at[12]).start()

            @pl.when(at.i != n)
            def _():
                send(dqv.at[n], block, send_sem.at[6], recv_sem.at[6], (at.member(n), e))

    class Reduce:
        def __init__(self, b):
            self.b = b
            self.copy = None
            self.x_ring = scatter_ring(
                4 + b, at.x, left_x, right_x,
                lambda q, h: part.at[b, q, pl.ds(64 * h, 64)], x_held.at[b],
            )

        def block(self, x, core):
            return pl.ds(pl.multiple_of((self.b * 8 + x * 2 + core) * TOK, TOK), TOK)

        def to_core(self):
            b = self.b

            def one(x, carry):
                core_out[b, x] = dlat[self.block(x, 1 - at.core), :].astype(BF16)
                return carry

            lax.fori_loop(0, 4, one, 0)
            self.copy = send(core_out.at[b], core_held.at[b], core_sem.at[b], core_sem.at[4 + b], sibling)

        def x1(self):
            b = self.b
            self.copy.wait_recv()

            def one(x, carry):
                part[b, x] = (dlat[self.block(x, at.core), :] + core_held[b, x].astype(F32)).astype(BF16)
                return carry

            lax.fori_loop(0, 4, one, 0)
            self.x_ring[0]()

        def x2(self):
            self.x_ring[1]()

        def x3(self):
            b = self.b
            self.x_ring[2]()
            for h in range(2):
                half = pl.ds(64 * h, 64)
                total = (
                    part[b, at.x, half].astype(F32) + x_held[b, 2 + h].astype(F32) + x_held[b, 4 + h].astype(F32)
                ).astype(BF16)
                for q in range(4):
                    y_part[b, q, half] = total[:, q * 128 : (q + 1) * 128]
            for k in range(1, 4):
                q = (at.y + k) % 4
                send(
                    y_part.at[b, q], y_held.at[b, k - 1], ring_send.at[8 + b, k], ring_recv.at[8 + b, k],
                    at.exp(q, at.zh),
                )

        def y3(self):
            b = self.b
            total = y_part[b, at.y].astype(F32)
            for k in range(3):
                drain(y_held.at[b, k], ring_recv.at[8 + b, k + 1])
                total = total + y_held[b, k].astype(F32)
            z_part[b] = total.astype(BF16)

    rs = [Reduce(b) for b in range(4)]

    def slice_lanes(n, f):
        return pl.ds(pl.multiple_of(n * 896 + f * 128, 128), 128)

    def slice_all(n):
        return pl.ds(pl.multiple_of(n * 896, 128), 896)

    def experts():
        for k in (6, 7, 8):
            own[k].wait()

        def unpack(n, carry):
            spread[...] = rows[n].reshape(1024, 128).astype(F32)
            for k in range(2):
                for f in range(7):
                    m = k * 7 + f
                    xs[32 * k : 32 * k + 32, slice_lanes(n, f)] = spread[pl.ds(m, 32, stride=32), :].astype(BF16)
                    ys[32 * k : 32 * k + 32, slice_lanes(n, f)] = spread[pl.ds(14 + m, 32, stride=32), :].astype(BF16)
            return carry

        lax.fori_loop(0, 8, unpack, 0)
        gate = jnp.concatenate([spread[pl.ds(28, 32, stride=32), :], spread[pl.ds(29, 32, stride=32), :]], axis=0)

        def hidden(n, sums):
            a, b, d = sums
            x, dy = xs[:, slice_all(n)], ys[:, slice_all(n)]
            a = a + jnp.dot(x, wg[slice_all(n), :], preferred_element_type=F32)
            b = b + jnp.dot(x, wu[slice_all(n), :], preferred_element_type=F32)
            d = d + lax.dot_general(dy, wd[:, slice_all(n)], contract_last, preferred_element_type=F32)
            return a, b, d

        zero = jnp.zeros((64, 128), F32)
        h1, h2, da = lax.fori_loop(0, 8, hidden, (zero, zero, zero))
        s = 1.0 / (1.0 + jnp.exp(-h1))
        act = h1 * s * h2
        gate_part = jnp.broadcast_to(jnp.sum(da * act, axis=1, keepdims=True), (64, 128))
        scaled = gate * da
        dh[0] = (gate * act).astype(BF16)
        dh[1] = (scaled * h2 * s * (1.0 + h1 * (1.0 - s))).astype(BF16)
        dh[2] = (scaled * h1 * s).astype(BF16)
        gate_sum[...] = gate_part

    def experts_back():
        for k in range(2):
            spread[pl.ds(14 + k, 32, stride=16), :] = gate_sum[32 * k : 32 * k + 32, :]

        def back(n, carry):
            dx = lax.dot_general(dh[1], wg[slice_all(n), :], contract_last, preferred_element_type=F32)
            dx = dx + lax.dot_general(dh[2], wu[slice_all(n), :], contract_last, preferred_element_type=F32)
            for k in range(2):
                for f in range(7):
                    spread[pl.ds(k * 7 + f, 32, stride=16), :] = dx[32 * k : 32 * k + 32, f * 128 : (f + 1) * 128]
            m_part[n] = spread[0:512, :].reshape(NC, 16, 128).astype(BF16)
            return carry

        lax.fori_loop(0, 8, back, 0)

    def weight_grads(out, k, dst, sem):
        def one(n, carry):
            out[slice_all(n), :] = lax.dot_general(
                xs[:, slice_all(n)], dh[k], contract_first, preferred_element_type=F32
            ).astype(BF16)
            return carry

        lax.fori_loop(0, 8, one, 0)
        copy = pltpu.make_async_copy(out, dst, sem)
        copy.start()
        return copy

    def down_grads():
        def one(n, carry):
            gwd[:, slice_all(n)] = lax.dot_general(
                dh[0], ys[:, slice_all(n)], contract_first, preferred_element_type=F32
            ).astype(BF16)
            return carry

        lax.fori_loop(0, 8, one, 0)
        copy = pltpu.make_async_copy(gwd, gwdo, own_sem.at[11])
        copy.start()
        return copy

    def y_total(h, k):
        return m_part[2 * at.y + h, k].astype(F32) + m_held[2 + h, k].astype(F32) + m_held[4 + h, k].astype(F32)

    def sum_rows(k, carry):
        for h in range(2):
            m_send[h, k] = y_total(h, k).astype(BF16)
        return carry

    def send_back(k, carry):
        d = (c + 1 + k) % NC
        send(m_send.at[at.zh, d], mo.at[at.zh, c], send_sem.at[5], recv_sem.at[5], (d, e))
        send(m_send.at[1 - at.zh, d], mo.at[at.zh, c], send_sem.at[8], recv_sem.at[8], (d, e_far))
        return carry

    def rows_back():
        mr[2]()
        lax.fori_loop(0, NC, sum_rows, 0)
        pltpu.make_async_copy(m_send.at[at.zh, c], mo.at[at.zh, c], own_sem.at[15]).start()
        lax.fori_loop(0, NC - 1, send_back, 0)
        send(m_send.at[1 - at.zh, c], mo.at[at.zh, c], send_sem.at[8], recv_sem.at[8], (c, e_far))

    def spread_weights():
        for i in range(8):
            for p in range(4):
                group = p if i % 2 == 0 else 3 - p
                rows16 = pl.ds(16 * (4 * i + p), 16)
                kq[group, i, 0] = kgv[rows16]
                kq[group, i, 1] = vgv[rows16]
        for k in range(1, 4):
            device, group = local(k)
            send(kq.at[group], kr.at[k - 1], local_send.at[2 + k], local_recv.at[2 + k], device)

    def return_weights():
        for k in range(3):
            drain(kr.at[k], local_recv.at[3 + k])

        def one(i, carry):
            ks[i] = (kq[at.r, i] + kr[0, i]) + (kr[1, i] + kr[2, i])
            return carry

        lax.fori_loop(0, 8, one, 0)
        pltpu.make_async_copy(ks.at[at.i], kv_held.at[at.i], own_sem.at[13]).start()

        def out(k, carry):
            i = (at.i + 1 + k) % 8
            send(ks.at[i], kv_held.at[at.i], send_sem.at[7], recv_sem.at[7], (at.member(i), e))
            return carry

        lax.fori_loop(0, 7, out, 0)

    kept = []

    chunk(3, after_output=(rows_here,))
    rs[3].to_core()
    chunk(2, after_score=(rs[3].x1, my[1]), after_output=(rs[3].x2,))
    rs[2].to_core()
    chunk(1, after_score=(rs[2].x1, rs[3].x3), after_output=(rs[2].x2,))
    rs[1].to_core()
    rs[3].y3()
    chunk(0, after_score=(rs[1].x1, rs[2].x3), after_output=(rs[1].x2,))
    rs[0].to_core()
    spread_weights()
    my[2]()
    experts()
    rs[0].x1()
    rs[2].y3()
    rs[1].x3()
    experts_back()
    mr[0]()
    rs[0].x2()
    return_weights()
    rs[1].y3()
    kept.append(down_grads())
    mr[1]()
    rs[0].x3()
    kept.append(weight_grads(gwg, 1, gwgo, own_sem.at[9]))
    rows_back()
    rs[0].y3()
    for k in range(1, 8):
        place = (at.zh * 4 + at.z + k) % 8
        z = place % 4
        device = (z * 8 + c % 8, at.y * 2 + place // 4)
        send(z_part.at[z], z_held.at[k - 1], last_send.at[k - 1], last_recv.at[k - 1], device)
    kept.append(weight_grads(gwu, 2, gwuo, own_sem.at[10]))

    drain(ks.at[0], own_sem.at[13])
    drain(ks.at[pl.ds(0, 7)], recv_sem.at[7])
    for n, out in ((0, kgo), (1, vgo)):
        for h in range(8):
            out[:, h * HD : (h + 1) * HD] = kv_held[h, n]
    total = z_part[at.z].astype(F32)
    for k in range(7):
        drain(z_held.at[k], last_recv.at[k])
        total = total + z_held[k].astype(F32)
    dlo[...] = jnp.where(at.zh == 0, total[:, :64], total[:, 64:]).T

    for copy in kept:
        copy.wait()
    for k in range(7):
        drain(z_held.at[k], last_send.at[k])
    for b in range(4):
        rs[b].copy.wait_send()
        for k in range(3):
            drain(y_held.at[b, k], ring_send.at[8 + b, k + 1])
    for k in range(3):
        drain(lat_own, z_send.at[k])
        drain(w4.at[at.r], local_send.at[k])
        drain(kr.at[k], local_send.at[3 + k])
    for k in range(8):
        drain(lat.at[pl.ds(0, 2), :, 0, :, pl.ds(0, 128)], piece_send.at[k])
    drain(rows.at[e, pl.ds(0, NC - 1)], send_sem.at[0])
    for k, ref in ((1, qv), (2, gv)):
        drain(ref.at[pl.ds(0, 7)], send_sem.at[k])
    for k in (3, 4):
        drain(w4.at[at.r, k - 3, pl.ds(0, 7)], send_sem.at[k])
    drain(m_send.at[0, 0], own_sem.at[15])
    drain(m_send.at[0, pl.ds(0, NC - 1)], send_sem.at[5])
    drain(m_send.at[0, pl.ds(0, NC - 1)], recv_sem.at[5])
    drain(m_send.at[0], send_sem.at[8])
    drain(m_send.at[0], recv_sem.at[8])
    drain(rows.at[e], send_sem.at[9])
    drain(dqv.at[0], own_sem.at[12])
    drain(dqv.at[pl.ds(0, 7)], send_sem.at[6])
    drain(dqv.at[pl.ds(0, 7)], recv_sem.at[6])
    drain(ks.at[pl.ds(0, 7)], send_sem.at[7])


def fused(queries, grad_heads, w_uk, w_uv, latents, messages, w_gate, w_up, w_down):
    anywhere = pl.BlockSpec(memory_space=pl.ANY)
    whole = pl.BlockSpec(memory_space=VMEM)
    shape = jax.ShapeDtypeStruct
    return pl.pallas_call(
        fused_kernel,
        out_shape=(
            shape((TOK, 8 * HD), BF16),
            shape((64, TOK), F32),
            shape((16, 8 * HD), F32),
            shape((16, 8 * HD), F32),
            shape((2, NC, 16, 128), BF16),
            shape((7168, 128), BF16),
            shape((7168, 128), BF16),
            shape((128, 7168), BF16),
        ),
        in_specs=[anywhere] * 9,
        out_specs=(anywhere, whole, whole, whole, anywhere, anywhere, anywhere, anywhere),
        scratch_shapes=[
            VMEM((4, 4, 2, TOK, 512), BF16),
            VMEM((512, 4096), BF16),
            VMEM((4096, 256), F32),
            VMEM((4096, 256), F32),
            VMEM((8, 8, 256), F32),
            VMEM((512, 256), F32),
            VMEM((512, 256), F32),
            VMEM((4096, 512), F32),
            VMEM((8, TOK, HD), BF16),
            VMEM((8, TOK, HD), BF16),
            VMEM((4, 2, 8, 16, HD), BF16),
            VMEM((512, HD), BF16),
            VMEM((512, HD), BF16),
            VMEM((8, TOK, HD), BF16),
            VMEM((512, HD), F32),
            VMEM((512, HD), F32),
            VMEM((4, 8, 2, 16, HD), F32),
            VMEM((3, 8, 2, 16, HD), F32),
            VMEM((8, 2, 16, HD), F32),
            VMEM((8, 2, 16, HD), F32),
            VMEM((4, 4, TOK, 512), BF16),
            VMEM((4, 4, TOK, 512), BF16),
            VMEM((4, 4, TOK, 512), BF16),
            VMEM((4, 6, 64, 512), BF16),
            VMEM((4, 4, TOK, 128), BF16),
            VMEM((4, 3, TOK, 128), BF16),
            VMEM((4, TOK, 128), BF16),
            VMEM((7, TOK, 128), BF16),
            VMEM((8, NC, 32, 128), BF16),
            VMEM((1024, 128), F32),
            VMEM((64, 7168), BF16),
            VMEM((64, 7168), BF16),
            VMEM((7168, 128), BF16),
            VMEM((7168, 128), BF16),
            VMEM((128, 7168), BF16),
            VMEM((7168, 128), BF16),
            VMEM((7168, 128), BF16),
            VMEM((128, 7168), BF16),
            VMEM((3, 64, 128), BF16),
            VMEM((8, NC, 16, 128), BF16),
            VMEM((6, NC, 16, 128), BF16),
            VMEM((2, NC, 16, 128), BF16),
            VMEM((64, 128), F32),
            DMA((16,)), DMA((10,)), DMA((10,)), DMA((7,)), DMA((7,)),
            DMA((14, 6)), DMA((14, 6)), DMA((8,)), DMA((7,)), DMA((7,)),
            DMA((8,)), DMA((8,)), DMA((6,)), DMA((6,)),
        ],
        compiler_params=pltpu.CompilerParams(
            collective_id=0, has_side_effects=True, vmem_limit_bytes=62 * 1024 * 1024
        ),
    )(queries, grad_heads, w_uk, w_uv, latents, messages, w_gate, w_up, w_down)


def finish_kernel(
    dq_in, dl_in, kg_in, vg_in, mo_in, wg_in, wu_in, wd_in, select_ref, dest_ref,
    dq_out, dl_out, kg_out, vg_out, moe_out, gate_out, wg_out, wu_out, wd_out,
    spread, slots, wg, wu, wd, sem,
):
    ins, outs = [], []
    for n, (src, held, dst) in enumerate(((wg_in, wg, wg_out), (wu_in, wu, wu_out), (wd_in, wd, wd_out))):
        size = src.shape[0] // 4
        for k in range(4):
            part = pl.ds(k * size, size)
            ins.append(pltpu.make_async_copy(src.at[part], held.at[part], sem.at[4 * n + k]))
            outs.append(pltpu.make_async_copy(held.at[part], dst.at[part], sem.at[12 + 4 * n + k]))
    for copy in ins:
        copy.start()
    for src, dst in ((dq_in, dq_out), (dl_in, dl_out), (kg_in, kg_out), (vg_in, vg_out)):
        dst[...] = src[...]
    for before, after in zip(ins, outs):
        before.wait()
        after.start()
    spread[...] = mo_in[...].reshape(1024, 128).astype(F32)

    def by_slot(row, step):
        for k in range(CAP):
            slots[pl.ds(k, 64, stride=2), :] = spread[pl.ds(row + k * step, 64, stride=16), :]
        return slots[...].astype(BF16)

    select = select_ref[...]
    twice = jnp.concatenate([select, select], axis=1)
    for f in range(7):
        moe_out[:, f * 128 : (f + 1) * 128] = jnp.dot(
            twice, by_slot(f, 7), preferred_element_type=F32
        ).astype(BF16)
    gates = by_slot(14, 1)
    lane = lax.broadcasted_iota(jnp.int32, (TOK, 128), 1)
    total = jnp.zeros((TOK, 128), F32)
    for j in range(8):
        hit = (dest_ref[:, j : j + 1] == lane % 64).astype(F32).astype(BF16)
        total = jnp.where(lane == j, jnp.dot(hit, gates, preferred_element_type=F32), total)
    gate_out[...] = total.T[0:8, :]
    for copy in outs:
        copy.wait()


def finish(dq, dl, kg, vg, mo, wg, wu, wd, select, dest):
    anywhere = pl.BlockSpec(memory_space=pl.ANY)
    whole = pl.BlockSpec(memory_space=VMEM)
    shape = jax.ShapeDtypeStruct
    return pl.pallas_call(
        finish_kernel,
        out_shape=(
            shape(dq.shape, BF16),
            shape(dl.shape, F32),
            shape(kg.shape, F32),
            shape(vg.shape, F32),
            shape((TOK, 896), BF16),
            shape((8, TOK), F32),
            shape(wg.shape, BF16),
            shape(wu.shape, BF16),
            shape(wd.shape, BF16),
        ),
        in_specs=[whole] * 5 + [anywhere] * 3 + [whole] * 2,
        out_specs=(whole,) * 6 + (anywhere,) * 3,
        scratch_shapes=[
            VMEM((1024, 128), F32),
            VMEM((128, 128), F32),
            VMEM(wg.shape, BF16),
            VMEM(wu.shape, BF16),
            VMEM(wd.shape, BF16),
            DMA((24,)),
        ],
        compiler_params=pltpu.CompilerParams(vmem_limit_bytes=62 * 1024 * 1024),
    )(dq, dl, kg, vg, mo, wg, wu, wd, select, dest)


def on_device(
    queries, grad_heads, latents, w_uk, w_uv, moe_in, grad_out, routes, slots, gates, w_gate, w_up, w_down
):
    slot_count = NC * CAP
    destination = jnp.where(slots >= 0, routes * CAP + slots, -1)
    matches = (
        destination[:, :, None] == jnp.arange(slot_count, dtype=jnp.int32)[None, None, :]
    ).astype(F32)
    selector = jnp.sum(matches, axis=1)
    selector_low = selector.astype(BF16)
    pick = (((0,), (0,)), ((), ()))
    rows_send = lax.dot_general(selector_low, moe_in, pick, preferred_element_type=F32).astype(BF16)
    grads_send = lax.dot_general(selector_low, grad_out, pick, preferred_element_type=F32).astype(BF16)
    gate_send = jnp.sum(matches * gates.astype(F32)[:, :, None], axis=(0, 1)).astype(BF16)
    messages = jnp.concatenate(
        [
            rows_send.reshape(NC, 14, 128),
            grads_send.reshape(NC, 14, 128),
            jnp.broadcast_to(gate_send.reshape(NC, CAP, 1), (NC, CAP, 128)),
            jnp.zeros((NC, 2, 128), BF16),
        ],
        axis=1,
    )
    results = fused(
        queries, grad_heads, w_uk, w_uv, latents, messages, w_gate[0], w_up[0], w_down[0]
    )
    (
        d_queries, d_latents, key_summed, value_summed, moe_grad, gate_grads, gate_wgrad, up_wgrad, down_grad,
    ) = finish(*results, selector_low, destination)
    return (
        d_queries, d_latents.T, key_summed, value_summed, moe_grad, gate_grads.T,
        gate_wgrad[None], up_wgrad[None], down_grad[None],
    )


def solution(mesh):
    rows = P("ctx", "exp")
    in_specs = (
        rows, rows, P("ctx", None), rows, rows, rows, rows, P("ctx", None), P("ctx", None), P("ctx", None),
        P("ctx", None, "exp"), P("ctx", None, "exp"), P("ctx", "exp", None),
    )
    out_specs = (
        rows, rows, rows, rows, rows, P("ctx", None),
        P("ctx", None, "exp"), P("ctx", None, "exp"), P("ctx", "exp", None),
    )
    return jax.shard_map(on_device, mesh=mesh, in_specs=in_specs, out_specs=out_specs, check_vma=False)
```

```python
import jax
import jax.numpy as jnp
from jax import lax
from jax.experimental import pallas as pl
from jax.experimental.pallas import tpu as pltpu
from jax.sharding import PartitionSpec as P

MESH = pl.DeviceIdType.MESH
HD = 128
CAP = 2
TOK = 128
NC = 32
F32 = jnp.float32
BF16 = jnp.bfloat16
DMA = pltpu.SemaphoreType.DMA
VMEM = pltpu.VMEM


class Place:
    def __init__(self):
        self.c = c = lax.axis_index("ctx")
        self.e = e = lax.axis_index("exp")
        self.z, self.x, self.core = c // 8, (c // 2) % 4, c % 2
        self.y, self.zh = e // 2, e % 2
        p = c % 8
        self.i = c // 4
        self.r = p + (p // 4) * (7 - 2 * p)

    def ctx(self, z, x, core):
        return (z * 8 + x * 2 + core, self.e)

    def exp(self, y, zh):
        return (self.c, y * 2 + zh)

    def member(self, i):
        return 4 * i + self.r + (i % 2) * (3 - 2 * self.r)


def greet(devices, loops):
    barrier = pltpu.get_barrier_semaphore()
    count = 0
    for steps, device in loops:

        def one(k, carry, device=device):
            pl.semaphore_signal(barrier, inc=1, device_id=device(k), device_id_type=MESH)
            return carry

        lax.fori_loop(0, steps, one, 0)
        count += steps
    for device in devices:
        pl.semaphore_signal(barrier, inc=1, device_id=device, device_id_type=MESH)
    pl.semaphore_wait(barrier, count + len(devices))


def send(src, dst, send_sem, recv_sem, device):
    copy = pltpu.make_async_remote_copy(
        src_ref=src,
        dst_ref=dst,
        send_sem=send_sem,
        recv_sem=recv_sem,
        device_id=device,
        device_id_type=MESH,
    )
    copy.start()
    return copy


def drain(ref, sem):
    pltpu.make_async_copy(ref, ref, sem).wait()


def ring_gather(at, pos, left, right, send_sem, recv_sem):
    other = (pos + 2) % 4
    before, after = (pos + 3) % 4, (pos + 1) % 4

    def first():
        for h in range(2):
            send(at(pos, h), at(pos, h), send_sem.at[h], recv_sem.at[h], right)
            send(at(pos, h), at(pos, h), send_sem.at[2 + h], recv_sem.at[2 + h], left)

    def second():
        drain(at(before, 0), recv_sem.at[0])
        send(at(before, 0), at(before, 0), send_sem.at[4], recv_sem.at[4], right)
        drain(at(after, 1), recv_sem.at[3])
        send(at(after, 1), at(after, 1), send_sem.at[5], recv_sem.at[5], left)

    def last(arrived=lambda k, q: None):
        drain(at(before, 1), recv_sem.at[1])
        arrived(1, before)
        drain(at(after, 0), recv_sem.at[2])
        arrived(2, after)
        drain(at(other, 0), recv_sem.at[4])
        drain(at(other, 1), recv_sem.at[5])
        arrived(3, other)
        for k in range(6):
            drain(at(pos, 0), send_sem.at[k])

    return first, second, last


def ring_scatter(at, pos, left, right, held, send_sem, recv_sem, add):
    other = (pos + 2) % 4
    before, after = (pos + 3) % 4, (pos + 1) % 4

    def first(ready=lambda q: None):
        ready(other)
        send(at(other, 0), held.at[0], send_sem.at[0], recv_sem.at[0], right)
        send(at(other, 1), held.at[1], send_sem.at[1], recv_sem.at[1], left)
        ready(after)
        send(at(after, 1), held.at[3], send_sem.at[2], recv_sem.at[3], right)
        ready(before)
        send(at(before, 0), held.at[4], send_sem.at[3], recv_sem.at[4], left)
        ready(pos)

    def second():
        drain(held.at[0], recv_sem.at[0])
        add(at(after, 0), held.at[0])
        send(at(after, 0), held.at[2], send_sem.at[4], recv_sem.at[2], right)
        drain(held.at[1], recv_sem.at[1])
        add(at(before, 1), held.at[1])
        send(at(before, 1), held.at[5], send_sem.at[5], recv_sem.at[5], left)

    def last():
        for k in range(2, 6):
            drain(held.at[k], recv_sem.at[k])
        for k in range(6):
            drain(held.at[k], send_sem.at[k])

    return first, second, last


def add_into(dst, src):
    if len(dst.shape) == 2:
        dst[...] = (dst[...].astype(F32) + src[...].astype(F32)).astype(dst.dtype)
        return

    def one(k, carry):
        dst[k] = (dst[k].astype(F32) + src[k].astype(F32)).astype(dst.dtype)
        return carry

    lax.fori_loop(0, dst.shape[0], one, 0)


def named_slots(route_ref, slot_ref):
    slot = slot_ref[...]
    return jnp.where(slot >= 0, route_ref[...] * CAP + slot, -1).astype(F32).T


def fused_kernel(
    q_ref, g_ref, wk_ref, wv_ref, lat_ref, x_ref, dy_ref, route_ref, slot_ref, gate_ref, wg_ref, wu_ref, wd_ref,
    dqo, dlo, kgo, vgo, mo, gwgo, gwuo, gwdo,
    lat, lat_t, probs, dprob, tops, o_t, dq_t, dlat, qv, gv, w4, wkv, wvv, dqv, kgv, vgv, kq, kr, ks, kv_held,
    core_out, core_held, part, x_held, y_part, y_held, z_part, z_held,
    rows, spread, xs, ys, wg, wu, wd, gwg, gwu, gwd, dh, m_part, m_held, m_send, gate_sum, moe_ref, by_slot,
    own_sem, send_sem, recv_sem, z_send, z_recv, ring_send, ring_recv, core_send, core_recv, last_send, last_recv,
    piece_send, piece_recv, local_send, local_recv,
):
    at = Place()
    c, e = at.c, at.e
    left_x, right_x = at.ctx(at.z, (at.x + 3) % 4, at.core), at.ctx(at.z, (at.x + 1) % 4, at.core)
    left_y, right_y = at.exp((at.y + 3) % 4, at.zh), at.exp((at.y + 1) % 4, at.zh)
    sibling = at.ctx(at.z, at.x, 1 - at.core)
    here = at.zh * 4 + at.z
    e_far = at.y * 2 + 1 - at.zh
    greet(
        [at.exp((at.y + k) % 4, at.zh) for k in range(1, 4)],
        ((NC - 1, lambda k: ((c + 1 + k) % NC, e)), (NC, lambda k: ((c + k) % NC, e_far))),
    )

    def lanes(h):
        return pl.ds(pl.multiple_of(h * HD, HD), HD)

    def local(k):
        p = (c % 4 + k) % 4
        return (4 * at.i + p, e), p + (at.i % 2) * (3 - 2 * p)

    def gather_ring(n, pos, left, right, ref_at):
        return ring_gather(ref_at, pos, left, right, ring_send.at[n], ring_recv.at[n])

    def scatter_ring(n, pos, left, right, ref_at, held):
        return ring_scatter(ref_at, pos, left, right, held, ring_send.at[n], ring_recv.at[n], add_into)

    own = [
        pltpu.make_async_copy(moe_ref.at[c], rows.at[e, c], own_sem.at[0]),
        pltpu.make_async_copy(lat_ref.at[:, lanes(at.y)], lat.at[at.z, at.x, at.core, :, lanes(at.y)], own_sem.at[1]),
        pltpu.make_async_copy(q_ref.at[:, lanes(at.i)], qv.at[at.i], own_sem.at[2]),
        pltpu.make_async_copy(g_ref.at[:, lanes(at.i)], gv.at[at.i], own_sem.at[3]),
        pltpu.make_async_copy(wk_ref.at[:, lanes(at.i)], w4.at[at.r, 0, at.i], own_sem.at[4]),
        pltpu.make_async_copy(wv_ref.at[:, lanes(at.i)], w4.at[at.r, 1, at.i], own_sem.at[5]),
        pltpu.make_async_copy(wg_ref, wg, own_sem.at[6]),
        pltpu.make_async_copy(wu_ref, wu, own_sem.at[7]),
        pltpu.make_async_copy(wd_ref, wd, own_sem.at[8]),
    ]
    for k in range(1, 6):
        own[k].start()
    lat_own = lat.at[at.z, at.x, at.core, :, lanes(at.y)]
    for k in range(1, 4):
        send(
            lat_ref.at[:, lanes(at.y)], lat_own, z_send.at[k - 1], z_recv.at[k - 1],
            at.ctx((at.z + k) % 4, at.x, at.core),
        )

    def send_rows(k, carry):
        d = (c + 1 + k) % NC
        send(moe_ref.at[d], rows.at[e, c], send_sem.at[0], recv_sem.at[0], (d, e))
        send(moe_ref.at[d], rows.at[e, c], send_sem.at[9], recv_sem.at[9], (d, e_far))
        return carry


    def send_weights(k, carry):
        i = (at.i + 1 + k) % 8
        d = (at.member(i), e)
        send(wk_ref.at[:, lanes(i)], w4.at[at.r, 0, at.i], send_sem.at[3], recv_sem.at[3], d)
        send(wv_ref.at[:, lanes(i)], w4.at[at.r, 1, at.i], send_sem.at[4], recv_sem.at[4], d)
        return carry

    def send_heads(k, carry):
        i = (at.i + 1 + k) % 8
        d = (at.member(i), e)
        send(q_ref.at[:, lanes(i)], qv.at[at.i], send_sem.at[1], recv_sem.at[1], d)
        send(g_ref.at[:, lanes(i)], gv.at[at.i], send_sem.at[2], recv_sem.at[2], d)
        return carry

    for k in (6, 7, 8):
        own[k].start()

    own[1].wait()
    for k in range(3):
        drain(lat_own, z_recv.at[k])
    xa = gather_ring(0, at.x, left_x, right_x, lambda q, h: lat.at[h, q, at.core, :, lanes(at.y)])
    yb = gather_ring(1, at.y, left_y, right_y, lambda q, h: lat.at[2 + h, at.x, at.core, :, lanes(q)])
    ya = gather_ring(2, at.y, left_y, right_y, lambda q, h: lat.at[h, :, at.core, :, lanes(q)])
    xb = gather_ring(3, at.x, left_x, right_x, lambda q, h: lat.at[2 + h, q, at.core])
    xa[0]()
    yb[0]()
    lax.fori_loop(0, 7, send_heads, 0)
    lax.fori_loop(0, 7, send_weights, 0)
    xa[1]()
    yb[1]()

    def piece_a(k, q):
        ref = lat.at[pl.ds(0, 2), :, at.core, :, lanes(q)]
        send(ref, ref, piece_send.at[k], piece_recv.at[k], sibling)

    def piece_b(k, q):
        ref = lat.at[pl.ds(2, 2), q, at.core]
        send(ref, ref, piece_send.at[4 + k], piece_recv.at[4 + k], sibling)

    xa[2]()
    ya[0]()
    piece_a(0, at.y)
    yb[2]()
    xb[0]()
    piece_b(0, at.x)
    lane = lax.broadcasted_iota(jnp.int32, (TOK, 128), 1).astype(F32)
    named = named_slots(route_ref, slot_ref)
    gate_of = gate_ref[...].astype(F32).T
    hits = jnp.zeros((TOK, 128), F32)
    gated = jnp.zeros((TOK, 128), F32)
    for j in range(8):
        hit = named[:, j : j + 1] == lane
        hits = hits + jnp.where(hit, 1.0, 0.0)
        gated = gated + jnp.where(hit, gate_of[:, j : j + 1], 0.0)
    hits, gated = hits.astype(BF16), gated.astype(BF16)

    def put(row, step, values):
        by_slot[...] = values
        for k in range(CAP):
            spread[pl.ds(row + k * step, NC, stride=32), :] = by_slot[pl.ds(k, NC, stride=2), :]

    pick = (((0,), (0,)), ((), ()))
    for f in range(7):
        cols = slice(f * 128, (f + 1) * 128)
        put(f, 7, lax.dot_general(hits, x_ref[:, cols], pick, preferred_element_type=F32))
        put(14 + f, 7, lax.dot_general(hits, dy_ref[:, cols], pick, preferred_element_type=F32))
    put(28, 1, lax.dot_general(gated, jnp.ones((TOK, 128), BF16), pick, preferred_element_type=F32))
    put(30, 1, jnp.zeros((128, 128), F32))
    moe_ref[...] = spread[...].reshape(NC, 32, 128).astype(BF16)
    own[0].start()
    lax.fori_loop(0, NC - 1, send_rows, 0)
    send(moe_ref.at[c], rows.at[e, c], send_sem.at[9], recv_sem.at[9], (c, e_far))
    ya[1]()
    xb[1]()
    for k in (4, 5):
        own[k].wait()
    for k in (3, 4):
        drain(w4.at[at.r, k - 3, pl.ds(0, 7)], recv_sem.at[k])
    for k in range(1, 4):
        send(w4.at[at.r], w4.at[at.r], local_send.at[k - 1], local_recv.at[k - 1], local(k)[0])
    ya[2](piece_a)
    xb[2](piece_b)
    for k in range(3):
        drain(w4.at[at.r], local_recv.at[k])
    for i in range(8):
        for p in range(4):
            group = p if i % 2 == 0 else 3 - p
            rows16 = pl.ds(16 * (4 * i + p), 16)
            wkv[rows16] = w4[group, 0, i]
            wvv[rows16] = w4[group, 1, i]
    for k in (2, 3):
        own[k].wait()
    for k, ref in ((1, qv), (2, gv)):
        drain(ref.at[pl.ds(0, 7)], recv_sem.at[k])

    my = gather_ring(12, at.y, left_y, right_y, lambda q, h: rows.at[2 * q + h])
    mr = scatter_ring(13, at.y, left_y, right_y, lambda q, h: m_part.at[2 * q + h], m_held)

    def rows_here():
        own[0].wait()
        drain(rows.at[e, pl.ds(0, NC - 1)], recv_sem.at[0])
        drain(rows.at[e_far], recv_sem.at[9])
        my[0]()

    scale = HD**-0.5
    fast = scale * 1.4426950408889634
    contract_last = (((1,), (1,)), ((), ()))
    contract_first = (((0,), (0,)), ((), ()))
    width = 512

    def tile(t):
        return pl.ds(pl.multiple_of(t * width, width), width)

    def keys_at(t):
        return lat[t // 2, pl.ds(2 * (t % 2), 2)].reshape(width, 512)

    def pieces(first):
        for k in range(first, first + 4):
            drain(lat.at[pl.ds(0, 2), :, 0, :, pl.ds(0, 128)], piece_recv.at[k])

    pieces(0)
    column = lax.broadcasted_iota(jnp.int32, (1, 256), 1)
    key_at = lax.broadcasted_iota(jnp.int32, (width, 1), 0)

    def chunk(j, after_score=(), after_output=()):
        q, g = qv[2 * j : 2 * j + 2].reshape(256, HD), gv[2 * j : 2 * j + 2].reshape(256, HD)
        q_lat = lax.dot_general(q, wkv[...], contract_last, preferred_element_type=F32).astype(BF16)
        g_lat = lax.dot_general(g, wvv[...], contract_last, preferred_element_type=F32).astype(BF16)
        position = column + jnp.where(column < TOK, (8 * j + at.r) * TOK, (8 * j + 6 - at.r) * TOK)

        def score(b, state, masked):
            top, total = state
            raw = []
            for t in (2 * b, 2 * b + 1):
                keys = keys_at(t)
                if j == 3:
                    lat_t[:, tile(t)] = keys.T
                s = lax.dot_general(keys, q_lat, contract_last, preferred_element_type=F32)
                if masked:
                    s = jnp.where(key_at + t * width <= position, s, -jnp.inf)
                raw.append(s)
                dprob[tile(t), :] = lax.dot_general(keys, g_lat, contract_last, preferred_element_type=F32)
            new_top = jnp.maximum(top, jnp.max(jnp.maximum(raw[0], raw[1]), axis=0, keepdims=True))
            total = total * jnp.exp2((top - new_top) * fast)
            for u in range(2):
                weight = jnp.exp2((raw[u] - new_top) * fast)
                probs[tile(2 * b + u), :] = weight
                total = total + jnp.sum(weight, axis=0, keepdims=True)
            tops[b] = jnp.broadcast_to(new_top, (8, 256))
            return new_top, total

        state = (jnp.full((1, 256), -1e30, F32), jnp.zeros((1, 256), F32))
        if j == 3:
            state = lax.fori_loop(0, 2, lambda b, s: score(b, s, False), state)
            pieces(4)
            state = score(2, state, False)
        elif j > 0:
            state = lax.fori_loop(0, j, lambda b, s: score(b, s, False), state)
        top, total = score(j, state, True)
        inverse = 1.0 / total
        for step in after_score:
            step()
        o_t[...] = jnp.zeros_like(o_t)
        dq_t[...] = jnp.zeros_like(dq_t)

        def output(b, delta):
            factor = jnp.exp2((tops[b][0:1, :] - top) * fast) * inverse
            sum_o = o_t[...]
            for t in (2 * b, 2 * b + 1):
                prob_low = (probs[tile(t), :] * factor).astype(BF16)
                sum_o = sum_o + jnp.dot(lat_t[:, tile(t)], prob_low, preferred_element_type=F32)
                delta = delta + jnp.sum(prob_low.astype(F32) * dprob[tile(t), :], axis=0, keepdims=True)
            o_t[...] = sum_o
            return delta

        delta = lax.fori_loop(0, j + 1, output, jnp.zeros((1, 256), F32))
        for step in after_output:
            step()

        def gradient(b, carry):
            factor = jnp.exp2((tops[b][0:1, :] - top) * fast) * inverse
            sum_q = dq_t[...]
            for t in (2 * b, 2 * b + 1):
                prob = probs[tile(t), :] * factor
                dscore = (prob * (dprob[tile(t), :] - delta) * scale).astype(BF16)
                sum_q = sum_q + jnp.dot(lat_t[:, tile(t)], dscore, preferred_element_type=F32)
                step = jnp.dot(dscore, q_lat, preferred_element_type=F32) + jnp.dot(
                    prob.astype(BF16), g_lat, preferred_element_type=F32
                )
                dlat[tile(t), :] = step if j == 3 else dlat[tile(t), :] + step
            dq_t[...] = sum_q
            return carry

        lax.fori_loop(0, j + 1, gradient, 0)
        dq_low = dq_t[...].astype(BF16)
        dq = lax.dot_general(dq_low, wkv[...], contract_first, preferred_element_type=F32).astype(BF16)
        dqv[2 * j : 2 * j + 2] = dq.reshape(2, TOK, HD)
        kg = jnp.dot(dq_low, q, preferred_element_type=F32)
        vg = jnp.dot(o_t[...].astype(BF16), g, preferred_element_type=F32)
        kgv[...] = kg if j == 3 else kgv[...] + kg
        vgv[...] = vg if j == 3 else vgv[...] + vg
        for n in (2 * j, 2 * j + 1):
            block = dqo.at[:, lanes(at.i)]

            @pl.when(at.i == n)
            def _():
                pltpu.make_async_copy(dqv.at[n], block, own_sem.at[12]).start()

            @pl.when(at.i != n)
            def _():
                send(dqv.at[n], block, send_sem.at[6], recv_sem.at[6], (at.member(n), e))

    class Reduce:
        def __init__(self, b):
            self.b = b
            self.x_ring = scatter_ring(
                4 + b, at.x, left_x, right_x,
                lambda q, h: part.at[b, q, pl.ds(64 * h, 64)], x_held.at[b],
            )

        def block(self, x, core):
            return pl.ds(pl.multiple_of((self.b * 8 + x * 2 + core) * TOK, TOK), TOK)

        def to_core(self):
            b = self.b

            for k in (2, 1, 3, 0):
                x = (at.x + k) % 4
                core_out[b, x] = dlat[self.block(x, 1 - at.core), :].astype(BF16)
                send(core_out.at[b, x], core_held.at[b, x], core_send.at[b, k], core_recv.at[b, k], sibling)

        def x1(self):
            b = self.b

            def ready(x):
                k = (x + 4 - at.x) % 4
                drain(core_held.at[b, x], core_recv.at[b, k])
                part[b, x] = (dlat[self.block(x, at.core), :] + core_held[b, x].astype(F32)).astype(BF16)

            self.x_ring[0](ready)

        def x2(self):
            self.x_ring[1]()

        def x3(self):
            b = self.b
            self.x_ring[2]()
            for h in range(2):
                half = pl.ds(64 * h, 64)
                total = (
                    part[b, at.x, half].astype(F32) + x_held[b, 2 + h].astype(F32) + x_held[b, 4 + h].astype(F32)
                ).astype(BF16)
                for q in range(4):
                    y_part[b, q, half] = total[:, q * 128 : (q + 1) * 128]
            for k in range(1, 4):
                q = (at.y + k) % 4
                send(
                    y_part.at[b, q], y_held.at[b, k - 1], ring_send.at[8 + b, k], ring_recv.at[8 + b, k],
                    at.exp(q, at.zh),
                )

        def y3(self):
            b = self.b
            total = y_part[b, at.y].astype(F32)
            for k in range(3):
                drain(y_held.at[b, k], ring_recv.at[8 + b, k + 1])
                total = total + y_held[b, k].astype(F32)
            z_part[b] = total.astype(BF16)
            for half in range(2):

                @pl.when(here != half * 4 + b)
                def _():
                    send(
                        z_part.at[b], z_held.at[here], last_send.at[2 * b + half], last_recv.at[here],
                        (b * 8 + c % 8, at.y * 2 + half),
                    )

    rs = [Reduce(b) for b in range(4)]

    def slice_lanes(n, f):
        return pl.ds(pl.multiple_of(n * 896 + f * 128, 128), 128)

    def slice_all(n):
        return pl.ds(pl.multiple_of(n * 896, 128), 896)

    def experts():
        for k in (6, 7, 8):
            own[k].wait()

        def unpack(n, carry):
            spread[...] = rows[n].reshape(1024, 128).astype(F32)
            for k in range(2):
                for f in range(7):
                    m = k * 7 + f
                    xs[32 * k : 32 * k + 32, slice_lanes(n, f)] = spread[pl.ds(m, 32, stride=32), :].astype(BF16)
                    ys[32 * k : 32 * k + 32, slice_lanes(n, f)] = spread[pl.ds(14 + m, 32, stride=32), :].astype(BF16)
            return carry

        lax.fori_loop(0, 8, unpack, 0)
        gate = jnp.concatenate([spread[pl.ds(28, 32, stride=32), :], spread[pl.ds(29, 32, stride=32), :]], axis=0)

        def hidden(n, sums):
            a, b, d = sums
            x, dy = xs[:, slice_all(n)], ys[:, slice_all(n)]
            a = a + jnp.dot(x, wg[slice_all(n), :], preferred_element_type=F32)
            b = b + jnp.dot(x, wu[slice_all(n), :], preferred_element_type=F32)
            d = d + lax.dot_general(dy, wd[:, slice_all(n)], contract_last, preferred_element_type=F32)
            return a, b, d

        zero = jnp.zeros((64, 128), F32)
        h1, h2, da = lax.fori_loop(0, 8, hidden, (zero, zero, zero))
        s = 1.0 / (1.0 + jnp.exp(-h1))
        act = h1 * s * h2
        gate_part = jnp.broadcast_to(jnp.sum(da * act, axis=1, keepdims=True), (64, 128))
        scaled = gate * da
        dh[0] = (gate * act).astype(BF16)
        dh[1] = (scaled * h2 * s * (1.0 + h1 * (1.0 - s))).astype(BF16)
        dh[2] = (scaled * h1 * s).astype(BF16)
        gate_sum[...] = gate_part

    def experts_back():
        for k in range(2):
            spread[pl.ds(14 + k, 32, stride=16), :] = gate_sum[32 * k : 32 * k + 32, :]

        def back(n, carry):
            dx = lax.dot_general(dh[1], wg[slice_all(n), :], contract_last, preferred_element_type=F32)
            dx = dx + lax.dot_general(dh[2], wu[slice_all(n), :], contract_last, preferred_element_type=F32)
            for k in range(2):
                for f in range(7):
                    spread[pl.ds(k * 7 + f, 32, stride=16), :] = dx[32 * k : 32 * k + 32, f * 128 : (f + 1) * 128]
            m_part[n] = spread[0:512, :].reshape(NC, 16, 128).astype(BF16)
            return carry

        lax.fori_loop(0, 8, back, 0)

    def weight_grads(out, k, dst, sem):
        def one(n, carry):
            out[slice_all(n), :] = lax.dot_general(
                xs[:, slice_all(n)], dh[k], contract_first, preferred_element_type=F32
            ).astype(BF16)
            return carry

        lax.fori_loop(0, 8, one, 0)
        copy = pltpu.make_async_copy(out, dst, sem)
        copy.start()
        return copy

    def down_grads():
        def one(n, carry):
            gwd[:, slice_all(n)] = lax.dot_general(
                dh[0], ys[:, slice_all(n)], contract_first, preferred_element_type=F32
            ).astype(BF16)
            return carry

        lax.fori_loop(0, 8, one, 0)
        copy = pltpu.make_async_copy(gwd, gwdo, own_sem.at[11])
        copy.start()
        return copy

    def y_total(h, k):
        return m_part[2 * at.y + h, k].astype(F32) + m_held[2 + h, k].astype(F32) + m_held[4 + h, k].astype(F32)

    def sum_rows(k, carry):
        for h in range(2):
            m_send[h, k] = y_total(h, k).astype(BF16)
        return carry

    def send_back(k, carry):
        d = (c + 1 + k) % NC
        send(m_send.at[at.zh, d], mo.at[at.zh, c], send_sem.at[5], recv_sem.at[5], (d, e))
        send(m_send.at[1 - at.zh, d], mo.at[at.zh, c], send_sem.at[8], recv_sem.at[8], (d, e_far))
        return carry

    def rows_back():
        mr[2]()
        lax.fori_loop(0, NC, sum_rows, 0)
        pltpu.make_async_copy(m_send.at[at.zh, c], mo.at[at.zh, c], own_sem.at[15]).start()
        lax.fori_loop(0, NC - 1, send_back, 0)
        send(m_send.at[1 - at.zh, c], mo.at[at.zh, c], send_sem.at[8], recv_sem.at[8], (c, e_far))

    def spread_weights():
        for i in range(8):
            for p in range(4):
                group = p if i % 2 == 0 else 3 - p
                rows16 = pl.ds(16 * (4 * i + p), 16)
                kq[group, i, 0] = kgv[rows16]
                kq[group, i, 1] = vgv[rows16]
        for k in range(1, 4):
            device, group = local(k)
            send(kq.at[group], kr.at[k - 1], local_send.at[2 + k], local_recv.at[2 + k], device)

    def return_weights():
        for k in range(3):
            drain(kr.at[k], local_recv.at[3 + k])

        def one(i, carry):
            ks[i] = (kq[at.r, i] + kr[0, i]) + (kr[1, i] + kr[2, i])
            return carry

        lax.fori_loop(0, 8, one, 0)
        pltpu.make_async_copy(ks.at[at.i], kv_held.at[at.i], own_sem.at[13]).start()

        def out(k, carry):
            i = (at.i + 1 + k) % 8
            send(ks.at[i], kv_held.at[at.i], send_sem.at[7], recv_sem.at[7], (at.member(i), e))
            return carry

        lax.fori_loop(0, 7, out, 0)

    kept = []

    chunk(3, after_score=(rows_here,))
    rs[3].to_core()
    my[1]()
    chunk(2, after_score=(rs[3].x1,), after_output=(rs[3].x2,))
    rs[2].to_core()
    chunk(1, after_score=(rs[2].x1, rs[3].x3, my[2], experts, experts_back, mr[0]), after_output=(rs[2].x2,))
    rs[1].to_core()
    mr[1]()
    rs[3].y3()
    chunk(0, after_score=(rs[1].x1, rs[2].x3), after_output=(rs[1].x2,))
    rs[0].to_core()
    spread_weights()
    rs[0].x1()
    rows_back()
    rs[2].y3()
    rs[1].x3()
    rs[0].x2()
    return_weights()
    kept.append(down_grads())
    rs[0].x3()
    rs[1].y3()
    kept.append(weight_grads(gwg, 1, gwgo, own_sem.at[9]))
    rs[0].y3()
    kept.append(weight_grads(gwu, 2, gwuo, own_sem.at[10]))
    drain(ks.at[0], own_sem.at[13])
    drain(ks.at[pl.ds(0, 7)], recv_sem.at[7])
    for n, out in ((0, kgo), (1, vgo)):
        for h in range(8):
            out[:, h * HD : (h + 1) * HD] = kv_held[h, n]
    total = z_part[at.z].astype(F32)
    for k in range(1, 8):
        p = (here + k) % 8
        drain(z_held.at[p], last_recv.at[p])
        total = total + z_held[p].astype(F32)
    dlo[...] = jnp.where(at.zh == 0, total[:, :64], total[:, 64:]).T

    for copy in kept:
        copy.wait()
    for b in range(4):
        for half in range(2):

            @pl.when(here != half * 4 + b)
            def _():
                drain(z_part.at[b], last_send.at[2 * b + half])
    for b in range(4):
        for k in range(4):
            drain(core_held.at[b, k], core_send.at[b, k])
        for k in range(3):
            drain(y_held.at[b, k], ring_send.at[8 + b, k + 1])
    for k in range(3):
        drain(lat_own, z_send.at[k])
        drain(w4.at[at.r], local_send.at[k])
        drain(kr.at[k], local_send.at[3 + k])
    for k in range(8):
        drain(lat.at[pl.ds(0, 2), :, 0, :, pl.ds(0, 128)], piece_send.at[k])
    drain(rows.at[e, pl.ds(0, NC - 1)], send_sem.at[0])
    for k, ref in ((1, qv), (2, gv)):
        drain(ref.at[pl.ds(0, 7)], send_sem.at[k])
    for k in (3, 4):
        drain(w4.at[at.r, k - 3, pl.ds(0, 7)], send_sem.at[k])
    drain(m_send.at[0, 0], own_sem.at[15])
    drain(m_send.at[0, pl.ds(0, NC - 1)], send_sem.at[5])
    drain(m_send.at[0, pl.ds(0, NC - 1)], recv_sem.at[5])
    drain(m_send.at[0], send_sem.at[8])
    drain(m_send.at[0], recv_sem.at[8])
    drain(rows.at[e], send_sem.at[9])
    drain(dqv.at[0], own_sem.at[12])
    drain(dqv.at[pl.ds(0, 7)], send_sem.at[6])
    drain(dqv.at[pl.ds(0, 7)], recv_sem.at[6])
    drain(ks.at[pl.ds(0, 7)], send_sem.at[7])


def fused(queries, grad_heads, w_uk, w_uv, latents, moe_in, grad_out, routes, slots, gates, w_gate, w_up, w_down):
    anywhere = pl.BlockSpec(memory_space=pl.ANY)
    whole = pl.BlockSpec(memory_space=VMEM)
    shape = jax.ShapeDtypeStruct
    return pl.pallas_call(
        fused_kernel,
        out_shape=(
            shape((TOK, 8 * HD), BF16),
            shape((64, TOK), F32),
            shape((16, 8 * HD), F32),
            shape((16, 8 * HD), F32),
            shape((2, NC, 16, 128), BF16),
            shape((7168, 128), BF16),
            shape((7168, 128), BF16),
            shape((128, 7168), BF16),
        ),
        in_specs=[anywhere] * 5 + [whole] * 5 + [anywhere] * 3,
        out_specs=(anywhere, whole, whole, whole, anywhere, anywhere, anywhere, anywhere),
        scratch_shapes=[
            VMEM((4, 4, 2, TOK, 512), BF16),
            VMEM((512, 4096), BF16),
            VMEM((4096, 256), F32),
            VMEM((4096, 256), F32),
            VMEM((8, 8, 256), F32),
            VMEM((512, 256), F32),
            VMEM((512, 256), F32),
            VMEM((4096, 512), F32),
            VMEM((8, TOK, HD), BF16),
            VMEM((8, TOK, HD), BF16),
            VMEM((4, 2, 8, 16, HD), BF16),
            VMEM((512, HD), BF16),
            VMEM((512, HD), BF16),
            VMEM((8, TOK, HD), BF16),
            VMEM((512, HD), F32),
            VMEM((512, HD), F32),
            VMEM((4, 8, 2, 16, HD), F32),
            VMEM((3, 8, 2, 16, HD), F32),
            VMEM((8, 2, 16, HD), F32),
            VMEM((8, 2, 16, HD), F32),
            VMEM((4, 4, TOK, 512), BF16),
            VMEM((4, 4, TOK, 512), BF16),
            VMEM((4, 4, TOK, 512), BF16),
            VMEM((4, 6, 64, 512), BF16),
            VMEM((4, 4, TOK, 128), BF16),
            VMEM((4, 3, TOK, 128), BF16),
            VMEM((4, TOK, 128), BF16),
            VMEM((8, TOK, 128), BF16),
            VMEM((8, NC, 32, 128), BF16),
            VMEM((1024, 128), F32),
            VMEM((64, 7168), BF16),
            VMEM((64, 7168), BF16),
            VMEM((7168, 128), BF16),
            VMEM((7168, 128), BF16),
            VMEM((128, 7168), BF16),
            VMEM((7168, 128), BF16),
            VMEM((7168, 128), BF16),
            VMEM((128, 7168), BF16),
            VMEM((3, 64, 128), BF16),
            VMEM((8, NC, 16, 128), BF16),
            VMEM((6, NC, 16, 128), BF16),
            VMEM((2, NC, 16, 128), BF16),
            VMEM((64, 128), F32),
            VMEM((NC, 32, 128), BF16),
            VMEM((128, 128), F32),
            DMA((16,)), DMA((10,)), DMA((10,)), DMA((7,)), DMA((7,)),
            DMA((14, 6)), DMA((14, 6)), DMA((4, 4)), DMA((4, 4)), DMA((8,)), DMA((8,)),
            DMA((8,)), DMA((8,)), DMA((6,)), DMA((6,)),
        ],
        compiler_params=pltpu.CompilerParams(
            collective_id=0, has_side_effects=True, vmem_limit_bytes=62 * 1024 * 1024
        ),
    )(queries, grad_heads, w_uk, w_uv, latents, moe_in, grad_out, routes, slots, gates, w_gate, w_up, w_down)


def finish_kernel(
    dq_in, dl_in, kg_in, vg_in, mo_in, wg_in, wu_in, wd_in, route_ref, slot_ref,
    dq_out, dl_out, kg_out, vg_out, moe_out, gate_out, wg_out, wu_out, wd_out,
    spread, slots, wg, wu, wd, sem,
):
    ins, outs = [], []
    for n, (src, held, dst) in enumerate(((wg_in, wg, wg_out), (wu_in, wu, wu_out), (wd_in, wd, wd_out))):
        size = src.shape[0] // 4
        for k in range(4):
            part = pl.ds(k * size, size)
            ins.append(pltpu.make_async_copy(src.at[part], held.at[part], sem.at[4 * n + k]))
            outs.append(pltpu.make_async_copy(held.at[part], dst.at[part], sem.at[12 + 4 * n + k]))
    for copy in ins:
        copy.start()
    for src, dst in ((dq_in, dq_out), (dl_in, dl_out), (kg_in, kg_out), (vg_in, vg_out)):
        dst[...] = src[...]
    for before, after in zip(ins, outs):
        before.wait()
        after.start()
    spread[...] = mo_in[...].reshape(1024, 128).astype(F32)

    def by_slot(row, step):
        for k in range(CAP):
            slots[pl.ds(k, 64, stride=2), :] = spread[pl.ds(row + k * step, 64, stride=16), :]
        return slots[...].astype(BF16)

    gates = by_slot(14, 1)
    number = lax.broadcasted_iota(jnp.int32, (TOK, 128), 1)
    lane = (number % 64).astype(F32)
    named = named_slots(route_ref, slot_ref)
    total = jnp.zeros((TOK, 128), F32)
    hits = jnp.zeros((TOK, 128), F32)
    for j in range(8):
        hit = jnp.where(named[:, j : j + 1] == lane, 1.0, 0.0)
        hits = hits + hit
        total = jnp.where(number == j, jnp.dot(hit.astype(BF16), gates, preferred_element_type=F32), total)
    gate_out[...] = total.T[0:8, :]
    hits = hits.astype(BF16)
    for f in range(7):
        moe_out[:, f * 128 : (f + 1) * 128] = jnp.dot(hits, by_slot(f, 7), preferred_element_type=F32).astype(BF16)
    for copy in outs:
        copy.wait()


def finish(dq, dl, kg, vg, mo, wg, wu, wd, routes, slots):
    anywhere = pl.BlockSpec(memory_space=pl.ANY)
    whole = pl.BlockSpec(memory_space=VMEM)
    shape = jax.ShapeDtypeStruct
    return pl.pallas_call(
        finish_kernel,
        out_shape=(
            shape(dq.shape, BF16),
            shape(dl.shape, F32),
            shape(kg.shape, F32),
            shape(vg.shape, F32),
            shape((TOK, 896), BF16),
            shape((8, TOK), F32),
            shape(wg.shape, BF16),
            shape(wu.shape, BF16),
            shape(wd.shape, BF16),
        ),
        in_specs=[whole] * 5 + [anywhere] * 3 + [whole] * 2,
        out_specs=(whole,) * 6 + (anywhere,) * 3,
        scratch_shapes=[
            VMEM((1024, 128), F32),
            VMEM((128, 128), F32),
            VMEM(wg.shape, BF16),
            VMEM(wu.shape, BF16),
            VMEM(wd.shape, BF16),
            DMA((24,)),
        ],
        compiler_params=pltpu.CompilerParams(vmem_limit_bytes=62 * 1024 * 1024),
    )(dq, dl, kg, vg, mo, wg, wu, wd, routes, slots)


def on_device(
    queries, grad_heads, latents, w_uk, w_uv, moe_in, grad_out, routes, slots, gates, w_gate, w_up, w_down
):
    routes, slots = routes.T, slots.T
    results = fused(
        queries, grad_heads, w_uk, w_uv, latents, moe_in, grad_out, routes, slots, gates.T,
        w_gate[0], w_up[0], w_down[0],
    )
    (
        d_queries, d_latents, key_summed, value_summed, moe_grad, gate_grads, gate_wgrad, up_wgrad, down_grad,
    ) = finish(*results, routes, slots)
    return (
        d_queries, d_latents.T, key_summed, value_summed, moe_grad, gate_grads.T,
        gate_wgrad[None], up_wgrad[None], down_grad[None],
    )


def solution(mesh):
    rows = P("ctx", "exp")
    in_specs = (
        rows, rows, P("ctx", None), rows, rows, rows, rows, P("ctx", None), P("ctx", None), P("ctx", None),
        P("ctx", None, "exp"), P("ctx", None, "exp"), P("ctx", "exp", None),
    )
    out_specs = (
        rows, rows, rows, rows, rows, P("ctx", None),
        P("ctx", None, "exp"), P("ctx", None, "exp"), P("ctx", "exp", None),
    )
    return jax.shard_map(on_device, mesh=mesh, in_specs=in_specs, out_specs=out_specs, check_vma=False)
```
